128 devices in a mesh: gx: 16 (over y, x), gy: 8 (over z, core).
Axes of the slice: x: 4, y: 4, z: 4, core: 2. Of those that a mesh axis runs over, the one named last changes fastest.
Arguments:
- initial_latents: float32 [16, 8, 128, 128], P('gx', 'gy'), may hold values from -6 to 6
- final_cotangent: float32 [16, 8, 128, 128], P('gx', 'gy'), may hold values from -6 to 6
- bin_counts: int32 [16, 8], P('gx', 'gy'), may hold values from 32 to 128, as said below
- neighbours: int32 [16, 8, 128, 24], P('gx', 'gy'), may hold values from 0 to 1151, as said below
- leave_rows: int32 [16, 8, 128, 8], P('gx', 'gy'), may hold values from 0 to 127
- leave_counts: int32 [16, 8, 128], P('gx', 'gy'), may hold values from 0 to 8, as said below
- w_send: float32 [2, 128, 128], replicated, may hold values from -0.5 to 0.5
- w_receive: float32 [2, 128, 128], replicated, may hold values from -0.5 to 0.5
- w_edge: float32 [2, 128, 128], replicated, may hold values from -0.5 to 0.5
- w_node: float32 [2, 256, 128], replicated, may hold values from -0.375 to 0.375
- w_update: float32 [2, 128, 128], replicated, may hold values from -0.5 to 0.5
Outputs:
- final_latents: float32 [16, 8, 128, 128], P('gx', 'gy')
- arrivals: float32 [16, 8, 128, 8, 128], P('gx', 'gy')
- grad_initial: float32 [16, 8, 128, 128], P('gx', 'gy')
- grad_send: float32 [2, 128, 128], replicated
- grad_receive: float32 [2, 128, 128], replicated
- grad_edge: float32 [2, 128, 128], replicated
- grad_node: float32 [2, 256, 128], replicated
- grad_update: float32 [2, 128, 128], replicated
The draws below stay inside these ranges and needn't reach their ends.
Inputs may be any that keep to these rules, and one draw needn't show every extreme that they name: `bin_counts`: at least 32; bin (0, 0) holds 128. `neighbours`: each sender lies in the 3 x 3 bins around the receiver's bin, in the device's frame of (3) x (3) bins of 128 slots. `leave_counts`: zero from a device to itself; with devices numbered d = ix * 8 + iy, every device sends 8 particles to the device whose number is d plus half the number of devices, counted round.
All inputs are finite; a program needn't handle non-finite values.
Results may differ from the reference program's by a relative error of at most 0.00013.
Values sent between devices are 32-bit elements; how exact they have to be, the bound alone decides.
No kernel may reach another device: no remote copies, remote signals or barrier semaphores. Data moves between devices by JAX's collectives and lax.ppermute only.
A program may use at most 64 MiB of HBM per device.

```python
import jax
import jax.numpy as jnp
from jax import lax

D = 128
BIN = 128
K = 24
STEPS = 2
CAP = 8
BX = 1
BY = 1
ROWS_DEV = 128
GRID_X = 16
GRID_Y = 8
N_GX = 16
N_GY = 8


def draw_bin_counts(key, part):
    key = jax.random.fold_in(key, 11)
    drawn = jax.random.randint(key, (GRID_X, GRID_Y), BIN // 4, BIN + 1, dtype=jnp.int32)
    corner = (jnp.arange(GRID_X)[:, None] == 0) & (jnp.arange(GRID_Y)[None, :] == 0)
    return jnp.where(corner, BIN, drawn).astype(jnp.int32)


def draw_neighbours(key, part):
    key = jax.random.fold_in(key, 23)
    key_x, key_y, key_r = jax.random.split(key, 3)
    shape = (GRID_X, GRID_Y, BIN, K)
    offset_x = jax.random.randint(key_x, shape, 0, 3, dtype=jnp.int32)
    offset_y = jax.random.randint(key_y, shape, 0, 3, dtype=jnp.int32)
    slot_rows = jax.random.randint(key_r, shape, 0, BIN, dtype=jnp.int32)
    first = (jnp.arange(BIN) == 0)[None, None, :, None]
    last_k = (jnp.arange(K) == K - 1)[None, None, None, :]
    near_k = (jnp.arange(K) == K - 2)[None, None, None, :]
    top = first & last_k
    low = first & near_k
    offset_x = jnp.where(top, 2, jnp.where(low, 0, offset_x))
    offset_y = jnp.where(top, 2, jnp.where(low, 0, offset_y))
    slot_rows = jnp.where(top, BIN - 1, jnp.where(low, 0, slot_rows))
    local_x = (jnp.arange(GRID_X, dtype=jnp.int32) % BX)[:, None, None, None]
    local_y = (jnp.arange(GRID_Y, dtype=jnp.int32) % BY)[None, :, None, None]
    return (((local_x + offset_x) * (BY + 2) + local_y + offset_y) * BIN + slot_rows).astype(jnp.int32)


def draw_leave_counts(key, part):
    key = jax.random.fold_in(key, 37)
    devices = N_GX * N_GY
    drawn = jax.random.randint(key, (N_GX, N_GY, devices), 0, CAP + 1, dtype=jnp.int32)
    source = jnp.arange(N_GX, dtype=jnp.int32)[:, None, None] * N_GY + jnp.arange(N_GY, dtype=jnp.int32)[None, :, None]
    target = jnp.arange(devices, dtype=jnp.int32)[None, None, :]
    forced = target == (source + devices // 2) % devices
    itself = target == source
    return jnp.where(forced, CAP, jnp.where(itself, 0, drawn)).astype(jnp.int32)


def with_ends(array, key, low, top_value):
    extent = array.shape
    index_at = [jax.random.randint(jax.random.fold_in(key, axis), (), 0, extent[axis]) for axis in range(len(extent))]
    array = array.at[tuple(index_at)].set(low)
    longest = extent.index(max(extent))
    index_at[longest] = (index_at[longest] + 1) % extent[longest]
    return array.at[tuple(index_at)].set(top_value)


def shard_levels(key, extent, cuts, smallest, high):
    gain = 1.0
    for position, parts in cuts:
        draws = jax.random.uniform(jax.random.fold_in(jax.random.fold_in(key, 6), position), (parts,), jnp.float32, smallest / len(cuts), high / len(cuts))
        gain = gain * jnp.repeat(jnp.exp(draws), extent[position] // parts).reshape((-1,) + (1,) * (len(extent) - 1 - position))
    return gain


def noise(rng, extent, scale, limit, pieces=(), kind=jnp.bfloat16):
    array = scale * jax.random.normal(rng, extent, jnp.float32)
    if pieces:
        array = array * shard_levels(rng, extent, pieces, -0.22, 0.18)
    return jnp.clip(array, -limit, limit).astype(kind)


def setup_inputs(seed: int = 0) -> dict:
    seeds = jax.random.split(jax.random.key(seed), 12)
    return {
        "initial_latents": noise(seeds[0], (GRID_X, GRID_Y, BIN, D), 1.0, 6.0, ((0, 16), (1, 8)), jnp.float32),
        "final_cotangent": noise(seeds[1], (GRID_X, GRID_Y, BIN, D), 1.0, 6.0, ((0, 16), (1, 8)), jnp.float32),
        "bin_counts": draw_bin_counts(jax.random.fold_in(seeds[11], 71), 0),
        "neighbours": draw_neighbours(jax.random.fold_in(seeds[11], 71), 0),
        "leave_rows": with_ends(jax.random.randint(seeds[4], (N_GX, N_GY, N_GX * N_GY, CAP), 0, ROWS_DEV), jax.random.fold_in(seeds[4], 1), 0, ROWS_DEV - 1).astype(jnp.int32),
        "leave_counts": draw_leave_counts(jax.random.fold_in(seeds[11], 71), 0),
        "w_send": noise(seeds[6], (STEPS, D, D), D ** -0.5, 0.5, (), jnp.float32),
        "w_receive": noise(seeds[7], (STEPS, D, D), D ** -0.5, 0.5, (), jnp.float32),
        "w_edge": noise(seeds[8], (STEPS, D, D), D ** -0.5, 0.5, (), jnp.float32),
        "w_node": noise(seeds[9], (STEPS, 2 * D, D), (2 * D) ** -0.5, 0.375, (), jnp.float32),
        "w_update": noise(seeds[10], (STEPS, D, D), D ** -0.5, 0.5, (), jnp.float32),
    }


HIGH = lax.Precision.HIGHEST
EPS = 1e-05

def matmul(left, right):
    return jnp.dot(left, right, precision=HIGH, preferred_element_type=jnp.float32)

def normalize(values):
    centered = values - lax.optimization_barrier(jnp.mean(values, axis=-1, keepdims=True))
    return centered * lax.rsqrt(lax.optimization_barrier(jnp.mean(centered * centered, axis=-1, keepdims=True)) + EPS)

def messages(send_proj, send_valid, recv_proj, index, w_edge):
    hidden = jax.nn.silu(send_proj[index] + recv_proj[..., None, :])
    terms = matmul(hidden, w_edge) * send_valid[index][..., None]
    return lax.optimization_barrier(jnp.sum(terms, axis=-2))

def node_update(latents, message, valid, w_node, w_update):
    joined = jnp.concatenate([latents, message], axis=-1)
    inner = jax.nn.silu(matmul(joined, w_node))
    return latents + valid[..., None] * normalize(matmul(inner, w_update))

def global_index(neighbours):
    slot_rows = neighbours % BIN
    padded_bin = neighbours // BIN
    local_x = padded_bin // (BY + 2)
    local_y = padded_bin % (BY + 2)
    base_x = (jnp.arange(GRID_X, dtype=jnp.int32) // BX * BX)[:, None, None, None]
    base_y = (jnp.arange(GRID_Y, dtype=jnp.int32) // BY * BY)[None, :, None, None]
    return (((base_x + local_x) * (GRID_Y + 2) + base_y + local_y) * BIN + slot_rows).astype(jnp.int32)

def layer(latents, valid, padded_valid, index, weights):
    w_send, w_receive, w_edge, w_node, w_update = weights
    padded = jnp.pad(latents, ((1, 1), (1, 1), (0, 0), (0, 0)))
    send_proj = matmul(padded, w_send).reshape(-1, latents.shape[-1])
    recv_proj = matmul(latents, w_receive)
    edge_block = jax.checkpoint(lambda recv_block, index_block: messages(send_proj, padded_valid, recv_block, index_block, w_edge))
    message = lax.map(lambda couple: edge_block(couple[0], couple[1]), (recv_proj, index))
    return node_update(latents, message, valid, w_node, w_update)

def migrate(final, leave_rows, leave_counts):
    devices = N_GX * N_GY
    width = final.shape[-1]
    owned = final.reshape(N_GX, BX, N_GY, BY, BIN, width).transpose(0, 2, 1, 3, 4, 5).reshape(devices, BX * BY * BIN, width)
    chosen = leave_rows.reshape(devices, devices, CAP)
    picked = jax.vmap(lambda block, rows_of: block[rows_of])(owned, chosen)
    live = (jnp.arange(CAP, dtype=jnp.int32)[None, None, :] < leave_counts.reshape(devices, devices)[:, :, None]).astype(jnp.float32)
    picked = picked * live[..., None]
    return jnp.swapaxes(picked, 0, 1).reshape(N_GX, N_GY, devices, CAP, width)

def reference(initial_latents, final_cotangent, bin_counts, neighbours, leave_rows, leave_counts, w_send, w_receive, w_edge, w_node, w_update):
    slot_iota = jnp.arange(BIN, dtype=jnp.int32)
    valid = (slot_iota[None, None, :] < bin_counts[:, :, None]).astype(jnp.float32)
    padded_valid = jnp.pad(valid, ((1, 1), (1, 1), (0, 0))).reshape(-1)
    index = global_index(neighbours)

    def forward(latents, params):
        for layer_number in range(STEPS):
            latents = layer(latents, valid, padded_valid, index, tuple((p[layer_number] for p in params)))
        return latents
    params = (w_send, w_receive, w_edge, w_node, w_update)
    final, pullback = jax.vjp(forward, initial_latents, params)
    grad_initial, grads = pullback(final_cotangent)
    arrivals = migrate(final, leave_rows, leave_counts)
    return (final, arrivals, grad_initial, grads[0], grads[1], grads[2], grads[3], grads[4])
```

```python
import jax
import jax.numpy as jnp
from jax import lax
from jax.experimental import pallas as pl
from jax.experimental.pallas import tpu as pltpu
from jax.sharding import PartitionSpec as P

EPS = 1e-05
AXES = ("gx", "gy")
GX, GY = 16, 8
DEVICES = GX * GY
D = 128
R = 128
K = 24
BLOCKS = 9
CAP = 8
FLAG = 1e30
NEVER = -1e30
VMEM_BYTES = 48 * 1024 * 1024
F32, BF16 = jnp.float32, jnp.bfloat16


def halves(a):
    high = a.astype(BF16)
    return high, (a - high.astype(F32)).astype(BF16)


def fold(wide):
    n = wide.shape[1] // 2
    return wide[:, :n] + wide[:, n:]


def mm(a, b):
    ah, al = halves(a)
    bh, bl = halves(b)
    both = jnp.concatenate([bh, bl], 1)
    return fold(
        jnp.dot(
            jnp.concatenate([ah, al], 1),
            jnp.concatenate([both, both], 0),
            preferred_element_type=F32,
        )
    )


def mm_nt(a, b):
    return mm(a, b.T)


def mm_tn(a, b):
    ah, al = halves(a)
    bh, bl = halves(b)
    both = jnp.concatenate([bh, bl], 1)
    return fold(
        lax.dot_general(
            jnp.concatenate([ah, al], 0),
            jnp.concatenate([both, both], 0),
            (((0,), (0,)), ((), ())),
            preferred_element_type=F32,
        )
    )


def sigmoid(v):
    return 0.5 + 0.5 * jnp.tanh(0.5 * v)


def silu_and_slope(v):
    s = sigmoid(v)
    t = v * s
    return t, s + t * (1.0 - s)


def block_limits(flags):
    return [
        [
            jnp.where(((xs < 2) | (flags[1] > 0)) & ((ys < 2) | (flags[2] > 0)), 1e20, -1e20)
            for xs in range(3)
        ]
        for ys in range(3)
    ]


def one_hot(idx, k):
    column = lax.broadcast_in_dim(idx[:, k : k + 1], (R, BLOCKS * R), (0, 1))
    lanes = lax.broadcasted_iota(jnp.int32, (R, BLOCKS * R), 1)
    return jnp.where(column == lanes, 1.0, 0.0).astype(BF16)


def edge_forward(idx_ref, table_ref, receiver, slope_ref, wide):
    total = jnp.zeros((R, D), F32)
    for start in range(0, K, wide):
        hot = jnp.concatenate([one_hot(idx_ref[...], k) for k in range(start, start + wide)], 0)
        got = fold(jnp.dot(hot, table_ref[...], preferred_element_type=F32))
        for j in range(wide):
            t, slope = silu_and_slope(got[j * R : (j + 1) * R] + receiver)
            total = total + t
            slope_ref[start + j] = slope
    return total


def edge_backward(idxt_ref, slope_ref, back, terms_ref, outs):
    total = jnp.zeros((R, D), F32)
    for k in range(K):
        d = back * slope_ref[k]
        total = total + d
        high, low = halves(d)
        terms_ref[k * R : (k + 1) * R, 0:D] = high
        terms_ref[k * R : (k + 1) * R, D : 2 * D] = low
    for part in range(3):
        rows = lax.broadcasted_iota(jnp.int32, (3 * R, R), 0) + part * 3 * R
        hot = jnp.concatenate(
            [
                jnp.where(
                    lax.broadcast_in_dim(idxt_ref[k : k + 1, :], (3 * R, R), (0, 1)) == rows,
                    1.0,
                    0.0,
                ).astype(BF16)
                for k in range(K)
            ],
            1,
        )
        outs(part, fold(jnp.dot(hot, terms_ref[...], preferred_element_type=F32)))
    return total


def node_forward(h, message, live, w_node, w_update):
    a = mm(h, w_node[0:D]) + mm(message, w_node[D:])
    inner, slope = silu_and_slope(a)
    u = mm(inner, w_update)
    c = u - jnp.mean(u, axis=1, keepdims=True)
    scale = lax.rsqrt(jnp.mean(c * c, axis=1, keepdims=True) + EPS)
    n = c * scale
    return h + live * n, inner, slope, n, scale


def node_backward(dh, h, message, live, inner, slope, n, scale, w_node, w_update):
    dn = live * dh
    du = scale * (
        dn - jnp.mean(dn, axis=1, keepdims=True) - n * jnp.mean(dn * n, axis=1, keepdims=True)
    )
    g_update = mm_tn(inner, du)
    da = mm_nt(du, w_update) * slope
    g_low = mm_tn(h, da)
    g_high = mm_tn(message, da)
    dh_part = dh + mm_nt(da, w_node[0:D])
    dmessage = mm_nt(da, w_node[D:])
    return dh_part, dmessage, g_low, g_high, g_update


def live_rows(flags):
    rows = lax.broadcasted_iota(jnp.int32, (R, D), 0)
    return jnp.where(rows < flags[0], 1.0, 0.0)


def forward_0(
    flags, ta, to, tb, idx, h, w_send, w_recv, w_edge, w_node, w_update,
    h_out, send_out, recv_out, slope_out, sum_out, message_out, inner_out, islope_out, n_out, scale_out,
    table,
):
    limits = block_limits(flags)
    for ys, ref in enumerate((ta, to, tb)):
        for xs in range(3):
            hb = ref[xs]
            keep = hb < limits[ys][xs]
            sent = jnp.where(keep, mm(jnp.where(keep, hb, 0.0), w_send[0]), NEVER)
            high, low = halves(sent)
            at = (ys * 3 + xs) * R
            table[at : at + R, 0:D] = high
            table[at : at + R, D : 2 * D] = low
    live = live_rows(flags)
    h0 = h[...]
    hidden = edge_forward(idx, table, mm(h0, w_recv[0]), slope_out, 8)
    message = mm(hidden, w_edge[0])
    h1, inner, islope, n, scale = node_forward(h0, message, live, w_node[0], w_update[0])
    h_out[...] = h1
    send_out[...] = jnp.where(live > 0, mm(h1, w_send[1]), NEVER)
    recv_out[...] = mm(h1, w_recv[1])
    sum_out[...] = hidden
    message_out[...] = message
    inner_out[...] = inner
    islope_out[...] = islope
    n_out[...] = n
    scale_out[...] = lax.broadcast_in_dim(scale, (R, D), (0, 1))


def middle_1(
    flags, ta, to, tb, idx, idxt, h, recv, cot, w_recv, w_edge, w_node, w_update,
    h_out, pa, po, pb, dh_out, g_recv, g_edge, g_node, g_update,
    table, slope, terms,
):
    limits = block_limits(flags)
    for ys, ref in enumerate((ta, to, tb)):
        for xs in range(3):
            sent = jnp.where(limits[ys][xs] > 0, ref[xs], NEVER)
            high, low = halves(sent)
            at = (ys * 3 + xs) * R
            table[at : at + R, 0:D] = high
            table[at : at + R, D : 2 * D] = low
    live = live_rows(flags)
    h1 = h[...]
    hidden = edge_forward(idx, table, recv[...], slope, 8)
    message = mm(hidden, w_edge[1])
    h2, inner, islope, n, scale = node_forward(h1, message, live, w_node[1], w_update[1])
    h_out[...] = h2
    dh, dmessage, g_low, g_high, gu = node_backward(
        cot[...], h1, message, live, inner, islope, n, scale, w_node[1], w_update[1]
    )
    g_node[0:D] = g_low
    g_node[D:] = g_high
    g_update[...] = gu
    g_edge[...] = mm_tn(hidden, dmessage)

    def put(part, value):
        (pa, po, pb)[part][...] = value.reshape(3, R, D)

    drecv = edge_backward(idxt, slope, mm_nt(dmessage, w_edge[1]), terms, put)
    g_recv[...] = mm_tn(h1, drecv)
    dh_out[...] = dh + mm_nt(drecv, w_recv[1])


def backward_0(
    flags, ta, to, tb, idxt, ma, mo, mb, h_start, h, dh, slope, hidden, message, inner, islope, n, scale,
    w_send, w_recv, w_edge, w_node, w_update,
    pa, po, pb, dh_out, g_send1, g_send, g_recv, g_edge, g_node, g_update,
    terms,
):
    live = live_rows(flags)
    dsend = ma[...] + mo[...] + mb[...]
    g_send1[...] = mm_tn(h[...], dsend)
    dh1 = dh[...] + mm_nt(dsend, w_send[1])
    h0 = h_start[...]
    dh0, dmessage, g_low, g_high, gu = node_backward(
        dh1, h0, message[...], live, inner[...], islope[...], n[...], scale[:, 0:1], w_node[0], w_update[0]
    )
    g_node[0:D] = g_low
    g_node[D:] = g_high
    g_update[...] = gu
    g_edge[...] = mm_tn(hidden[...], dmessage)
    limits = block_limits(flags)
    gs = []
    back_w = w_send[0].T

    def put(part, value):
        ref = (ta, to, tb)[part]
        for xs in range(3):
            hb = ref[xs]
            v = value[xs * R : (xs + 1) * R]
            gs.append(mm_tn(jnp.where(hb < limits[part][xs], hb, 0.0), v))
            (pa, po, pb)[part][xs] = mm(v, back_w)

    drecv = edge_backward(idxt, slope, mm_nt(dmessage, w_edge[0]), terms, put)
    g_send[...] = sum(gs[1:], gs[0])
    g_recv[...] = mm_tn(h0, drecv)
    dh_out[...] = dh0 + mm_nt(drecv, w_recv[0])


def pack_leaving(rows, h, out):
    hot = jnp.where(
        lax.broadcasted_iota(jnp.int32, (R, DEVICES * CAP), 0)
        == lax.broadcast_in_dim(rows[...], (R, DEVICES * CAP), (0, 1)),
        1.0,
        0.0,
    ).astype(BF16)
    high, low = halves(h[...])
    got = fold(
        lax.dot_general(
            hot,
            jnp.concatenate([high, low], 1),
            (((0,), (0,)), ((), ())),
            preferred_element_type=F32,
        )
    )
    out[...] = got.reshape(DEVICES, CAP, D)


def call(kernel, outs, scratch, *args):
    smem = pl.BlockSpec(memory_space=pltpu.SMEM)
    vmem = pl.BlockSpec(memory_space=pltpu.VMEM)
    return pl.pallas_call(
        kernel,
        out_shape=[jax.ShapeDtypeStruct(s, F32) for s in outs],
        in_specs=[smem if a.ndim == 1 else vmem for a in args],
        out_specs=[vmem for _ in outs],
        scratch_shapes=scratch,
        compiler_params=pltpu.CompilerParams(vmem_limit_bytes=VMEM_BYTES),
    )(*args)


def swap(a, axis, second):
    n = lax.axis_size(axis)
    if second:
        pairs = [(i, (i + 1) % n if i % 2 else (i - 1) % n) for i in range(n)]
    else:
        pairs = [(i, i ^ 1) for i in range(n)]
    return lax.ppermute(a, axis, pairs)


def spread(own):
    first = swap(own, "gx", False)
    second = swap(own, "gx", True)
    column = jnp.stack([first, own, second])
    return swap(column, "gy", False), column, swap(column, "gy", True)


def collect(pa, po, pb):
    ra = swap(pa, "gy", False)
    rb = swap(pb, "gy", True)
    low = po[0] + ra[0] + rb[0]
    mid = po[1] + ra[1] + rb[1]
    high = po[2] + ra[2] + rb[2]
    return swap(low, "gx", False), mid, swap(high, "gx", True)


def body(
    initial_latents,
    final_cotangent,
    bin_counts,
    neighbours,
    leave_rows,
    leave_counts,
    w_send,
    w_receive,
    w_edge,
    w_node,
    w_update,
):
    gx, gy = lax.axis_index("gx"), lax.axis_index("gy")
    count = bin_counts[0, 0]
    flags = jnp.stack(
        [
            count,
            ((gx > 0) & (gx < GX - 1)).astype(jnp.int32),
            ((gy > 0) & (gy < GY - 1)).astype(jnp.int32),
            jnp.int32(0),
        ]
    )
    raw = neighbours[0, 0]
    place = raw // R
    px, py = place // 3, place % 3
    xs = jnp.where(gx % 2 == 0, 2 - px, px)
    ys = jnp.where(gy % 2 == 0, 2 - py, py)
    idx = (ys * 3 + xs) * R + raw % R
    idxt = idx.T
    h0 = initial_latents[0, 0]
    slots = lax.broadcasted_iota(jnp.int32, (R, D), 0)
    ta, to, tb = spread(jnp.where(slots < count, h0, FLAG))

    ta0, to0, tb0 = ta, to, tb
    row, table3, big = (R, D), (3, R, D), (K, R, D)
    (h1, send1, recv1, slope0, hidden0, message0, inner0, islope0, n0, scale0) = call(
        forward_0,
        [row, row, row, big, row, row, row, row, row, row],
        [pltpu.VMEM((BLOCKS * R, 2 * D), BF16)],
        flags, ta, to, tb, idx, h0, w_send, w_receive, w_edge, w_node, w_update,
    )
    ta, to, tb = spread(send1)
    wide = (2 * D, D)
    h2, pa, po, pb, dh1, g_recv1, g_edge1, g_node1, g_update1 = call(
        middle_1,
        [row, table3, table3, table3, row, row, row, wide, row],
        [
            pltpu.VMEM((BLOCKS * R, 2 * D), BF16),
            pltpu.VMEM(big, F32),
            pltpu.VMEM((K * R, 2 * D), BF16),
        ],
        flags, ta, to, tb, idx, idxt, h1, recv1, final_cotangent[0, 0], w_receive, w_edge, w_node, w_update,
    )
    ma, mo, mb = collect(pa, po, pb)
    (outgoing,) = call(
        pack_leaving,
        [(DEVICES, CAP, D)],
        [],
        jnp.where(
            lax.broadcasted_iota(jnp.int32, (DEVICES, CAP), 1) < leave_counts[0, 0][:, None],
            leave_rows[0, 0],
            -1,
        ).reshape(1, DEVICES * CAP),
        h2,
    )
    pa, po, pb, dh0, g_send1, g_send0, g_recv0, g_edge0, g_node0, g_update0 = call(
        backward_0,
        [table3, table3, table3, row, row, row, row, row, wide, row],
        [pltpu.VMEM((K * R, 2 * D), BF16)],
        flags, ta0, to0, tb0, idxt, ma, mo, mb, h0, h1, dh1, slope0, hidden0, message0, inner0, islope0, n0, scale0,
        w_send, w_receive, w_edge, w_node, w_update,
    )
    fa, fo, fb = collect(pa, po, pb)
    grad_initial = dh0 + fa + fo + fb
    grads = jnp.concatenate(
        [
            g_send0, g_send1, g_recv0, g_recv1, g_edge0, g_edge1, g_node0, g_node1, g_update0, g_update1,
        ],
        0,
    )
    pieces = grads.reshape(DEVICES, -1, D)
    arrived = lax.all_to_all(
        jnp.concatenate([outgoing, pieces], 1), AXES, split_axis=0, concat_axis=0, tiled=True
    )
    arrivals = arrived[:, :CAP]
    piece = jnp.sum(arrived[:, CAP:], axis=0, keepdims=True)
    summed = lax.all_to_all(
        jnp.broadcast_to(piece, pieces.shape), AXES, split_axis=0, concat_axis=0, tiled=True
    ).reshape(-1, D)
    o_send = summed[0:256].reshape(2, D, D)
    o_recv = summed[256:512].reshape(2, D, D)
    o_edge = summed[512:768].reshape(2, D, D)
    o_node = summed[768:1280].reshape(2, 2 * D, D)
    o_update = summed[1280:1536].reshape(2, D, D)
    return (
        h2.reshape(1, 1, R, D),
        arrivals.reshape(1, 1, DEVICES, CAP, D),
        grad_initial.reshape(1, 1, R, D),
        o_send,
        o_recv,
        o_edge,
        o_node,
        o_update,
    )


def solution(mesh):
    in_specs = (
        P("gx", "gy", None, None),
        P("gx", "gy", None, None),
        P("gx", "gy"),
        P("gx", "gy", None, None),
        P("gx", "gy", None, None),
        P("gx", "gy", None),
        P(),
        P(),
        P(),
        P(),
        P(),
    )
    out_specs = (
        P("gx", "gy", None, None),
        P("gx", "gy", None, None, None),
        P("gx", "gy", None, None),
        P(),
        P(),
        P(),
        P(),
        P(),
    )
    return jax.shard_map(body, mesh=mesh, in_specs=in_specs, out_specs=out_specs, check_vma=False)
```

```python
import jax
import jax.numpy as jnp
from jax import lax
from jax.experimental import pallas as pl
from jax.experimental.pallas import tpu as pltpu
from jax.sharding import PartitionSpec as P

EPS = 1e-05
AXES = ("gx", "gy")
GX, GY = 16, 8
DEVICES = GX * GY
CHIPS = DEVICES // 2
D = 128
R = 128
K = 24
BLOCKS = 9
CAP = 8
PIECE = 6 * D // CHIPS
SEND, RECV, EDGE, NODE, UPDATE = 0, 1, 2, 3, 5
FLAG = 1e30
NEVER = -1e30
VMEM_BYTES = 12 * 1024 * 1024
F32, BF16 = jnp.float32, jnp.bfloat16


def halves(a):
    high = a.astype(BF16)
    return high, (a - high.astype(F32)).astype(BF16)


def fold(wide):
    n = wide.shape[1] // 2
    return wide[:, :n] + wide[:, n:]


def pair(b):
    bh, bl = halves(b)
    both = jnp.concatenate([bh, bl], 1)
    return jnp.concatenate([both, both], 0)


def mm(a, paired):
    return fold(jnp.dot(jnp.concatenate(halves(a), 1), paired, preferred_element_type=F32))


def mm_tn(a, b):
    return fold(
        lax.dot_general(
            jnp.concatenate(halves(a), 0),
            pair(b),
            (((0,), (0,)), ((), ())),
            preferred_element_type=F32,
        )
    )


def sigmoid(v):
    return 0.5 + 0.5 * jnp.tanh(0.5 * v)


def silu_and_slope(v):
    s = sigmoid(v)
    t = v * s
    return t, s + t * (1.0 - s)


def block_limits(flags):
    return [
        [
            jnp.where(((xs < 2) | (flags[1] > 0)) & ((ys < 2) | (flags[2] > 0)), 1e20, -1e20)
            for xs in range(3)
        ]
        for ys in range(3)
    ]


def hot_rows(idx, k):
    column = lax.broadcast_in_dim(idx[:, k : k + 1], (R, BLOCKS * R), (0, 1))
    lanes = lax.broadcasted_iota(jnp.int32, (R, BLOCKS * R), 1)
    return jnp.where(column == lanes, 1.0, 0.0).astype(BF16)


def hot_columns(idxt, k, first, count):
    line = lax.broadcast_in_dim(idxt[k : k + 1, :], (count, R), (0, 1))
    rows = lax.broadcasted_iota(jnp.int32, (count, R), 0) + first
    return jnp.where(line == rows, 1.0, 0.0).astype(BF16)


def edge_forward(idx, table, receiver, slope_ref, wide):
    total = jnp.zeros((R, D), F32)
    for start in range(0, K, wide):
        hot = jnp.concatenate([hot_rows(idx, k) for k in range(start, start + wide)], 0)
        got = fold(jnp.dot(hot, table[...], preferred_element_type=F32))
        for j in range(wide):
            t, slope = silu_and_slope(got[j * R : (j + 1) * R] + receiver)
            total = total + t
            slope_ref[start + j] = slope
    return total


def edge_backward(idxt, slope_ref, back, terms_ref, outs):
    total = jnp.zeros((R, D), F32)
    for k in range(K):
        d = back * slope_ref[k]
        total = total + d
        high, low = halves(d)
        terms_ref[k * R : (k + 1) * R, 0:D] = high
        terms_ref[k * R : (k + 1) * R, D : 2 * D] = low
    for part in range(3):
        hot = jnp.concatenate([hot_columns(idxt, k, part * 3 * R, 3 * R) for k in range(K)], 1)
        outs(part, fold(jnp.dot(hot, terms_ref[...], preferred_element_type=F32)))
    return total


def node_forward(h, message, live, w, step):
    a = mm(h, w[step, NODE]) + mm(message, w[step, NODE + 1])
    inner, slope = silu_and_slope(a)
    u = mm(inner, w[step, UPDATE])
    c = u - jnp.mean(u, axis=1, keepdims=True)
    scale = lax.rsqrt(jnp.mean(c * c, axis=1, keepdims=True) + EPS)
    n = c * scale
    return h + live * n, inner, slope, n, scale


def node_backward(dh, h, message, live, inner, slope, n, scale, wt, step):
    dn = live * dh
    du = scale * (
        dn - jnp.mean(dn, axis=1, keepdims=True) - n * jnp.mean(dn * n, axis=1, keepdims=True)
    )
    da = mm(du, wt[step, UPDATE]) * slope
    dmessage = mm(da, wt[step, NODE + 1])
    back = mm(dmessage, wt[step, EDGE])
    dh_part = dh + mm(da, wt[step, NODE])
    g_update = mm_tn(inner, du)
    g_low = mm_tn(h, da)
    g_high = mm_tn(message, da)
    return dh_part, dmessage, back, g_low, g_high, g_update


def live_rows(flags):
    rows = lax.broadcasted_iota(jnp.int32, (R, D), 0)
    return jnp.where(rows < flags[0], 1.0, 0.0)


def prepare(flags, raw, send, recv, edge, node, update, h, cot, w, wt, idx, idxt, h_out, cot_out, f, sems):
    copies = [
        pltpu.make_async_copy(src, dst, sems.at[i])
        for i, (src, dst) in enumerate(
            (
                (send, f.at[:, 0:D]),
                (recv, f.at[:, D : 2 * D]),
                (edge, f.at[:, 2 * D : 3 * D]),
                (node, f.at[:, 3 * D : 5 * D]),
                (update, f.at[:, 5 * D : 6 * D]),
                (h, h_out),
                (cot, cot_out),
            )
        )
    ]
    for copy in copies:
        copy.start()
    place = raw[...] // R
    px = (place >= 3).astype(jnp.int32) + (place >= 6).astype(jnp.int32)
    py = place - 3 * px
    xs = jnp.where(flags[4] == 0, 2 - px, px)
    ys = jnp.where(flags[3] == 0, 2 - py, py)
    slot = (ys * 3 + xs) * R + raw[...] - place * R
    idxt[...] = slot
    tall = jnp.concatenate([slot.astype(F32), jnp.zeros((R - K, R), F32)], 0)
    idx[...] = tall.T.astype(jnp.int32)
    for copy in copies:
        copy.wait()
    for step in range(2):
        for m in range(6):
            v = f[step, m * D : (m + 1) * D]
            w[step, m] = pair(v)
            wt[step, m] = pair(v.T)


def fill(table, at, sent):
    high, low = halves(sent)
    table[at * R : (at + 1) * R, 0:D] = high
    table[at * R : (at + 1) * R, D : 2 * D] = low


def forward_0(flags, ta, to, tb, idx, h, w, send_out, saved, slope, bins, table):
    limits = block_limits(flags)
    for ys, ref in enumerate((ta, to, tb)):
        for xs in range(3):
            keep = ref[xs] < limits[ys][xs]
            b = jnp.where(keep, ref[xs], 0.0)
            bins[ys * 3 + xs] = b
            fill(table, ys * 3 + xs, jnp.where(keep, mm(b, w[0, SEND]), NEVER))
    live = live_rows(flags)
    h0 = h[...]
    hidden = edge_forward(idx, table, mm(h0, w[0, RECV]), slope, 8)
    message = mm(hidden, w[0, EDGE])
    h1, inner, islope, n, scale = node_forward(h0, message, live, w, 0)
    send_out[...] = jnp.where(live > 0, mm(h1, w[1, SEND]), NEVER)
    saved[0] = h1
    saved[1] = mm(h1, w[1, RECV])
    saved[2] = hidden
    saved[3] = message
    saved[4] = inner
    saved[5] = islope
    saved[6] = n
    saved[7] = lax.broadcast_in_dim(scale, (R, D), (0, 1))


def middle_1(
    flags, ta, to, tb, idx, idxt, saved, cot, w, wt, leave_rows, leave_counts,
    pa, pb, po, h_out, rows_keep, rows_send, g,
    table, slope, terms, h2, sem,
):
    limits = block_limits(flags)
    for ys, ref in enumerate((ta, to, tb)):
        for xs in range(3):
            fill(table, ys * 3 + xs, jnp.where(limits[ys][xs] > 0, ref[xs], NEVER))
    live = live_rows(flags)
    hidden = edge_forward(idx, table, saved[1], slope, 8)
    h1 = saved[0]
    message = mm(hidden, w[1, EDGE])
    new, inner, islope, n, scale = node_forward(h1, message, live, w, 1)
    h2[...] = new
    copy = pltpu.make_async_copy(h2, h_out, sem)
    copy.start()
    dh1, dmessage, back, g_low, g_high, gu = node_backward(
        cot[...], h1, message, live, inner, islope, n, scale, wt, 1
    )
    outs = (pa, po, pb)

    def put(part, value):
        outs[part][...] = value.reshape(3, R, D)

    drecv = edge_backward(idxt, slope, back, terms, put)
    g[0:D] = mm_tn(h1, drecv)
    g[D : 2 * D] = mm_tn(hidden, dmessage)
    g[2 * D : 3 * D] = g_low
    g[3 * D : 4 * D] = g_high
    g[4 * D : 5 * D] = gu
    g[5 * D :] = dh1 + mm(drecv, wt[1, RECV])
    pack_leaving(flags, leave_rows, leave_counts, new, rows_keep, rows_send)
    copy.wait()


def backward_0(
    flags, idxt, ma, mo, mb, saved, slope_in, bins_in, h, g1, wt,
    pa, pb, po, keep, send,
    terms, g, slope, bins, sems,
):
    slope_copy = pltpu.make_async_copy(slope_in, slope, sems.at[0])
    slope_copy.start()
    bins_copy = pltpu.make_async_copy(bins_in, bins, sems.at[1])
    bins_copy.start()
    live = live_rows(flags)
    dsend = ma[...] + mo[...] + mb[...]
    dh1 = g1[5 * D :] + mm(dsend, wt[1, SEND])
    h0 = h[...]
    dh0, dmessage, back, g_low, g_high, gu = node_backward(
        dh1, h0, saved[3], live, saved[4], saved[5], saved[6], saved[7][:, 0:1], wt, 0
    )
    gs = []
    outs = (pa, po, pb)

    def put(part, value):
        for xs in range(3):
            v = value[xs * R : (xs + 1) * R]
            gs.append(mm_tn(bins[part * 3 + xs], v))
            outs[part][xs] = mm(v, wt[0, SEND])

    slope_copy.wait()
    bins_copy.wait()
    drecv = edge_backward(idxt, slope, back, terms, put)
    g[0, 0:D] = sum(gs[1:], gs[0])
    g[0, D : 2 * D] = mm_tn(h0, drecv)
    g[0, 2 * D : 3 * D] = mm_tn(saved[2], dmessage)
    g[0, 3 * D : 4 * D] = g_low
    g[0, 4 * D : 5 * D] = g_high
    g[0, 5 * D :] = gu
    g[1, 0:D] = mm_tn(saved[0], dsend)
    g[1, D:] = g1[0 : 5 * D]
    mine = flags[3]
    keep[...] = g[mine]
    send[...] = g[1 - mine]
    po[1] += dh0 + mm(drecv, wt[0, RECV])


def pack_leaving(flags, rows, counts, h, keep, send):
    q = lax.broadcasted_iota(jnp.int32, (CAP, DEVICES), 0)
    rows = jnp.where(q < lax.broadcast_in_dim(counts[...], (CAP, DEVICES), (0, 1)), rows[...], -1)
    target = lax.broadcasted_iota(jnp.int32, (DEVICES, DEVICES), 0)
    at = lax.broadcasted_iota(jnp.int32, (DEVICES, DEVICES), 1)
    first = at < CHIPS
    wanted = jnp.where(first, 2 * at + flags[3], 2 * (at - CHIPS) + 1 - flags[3])
    order = jnp.where(target == wanted, 1.0, 0.0).astype(BF16)
    rows = jnp.dot(rows.astype(F32).astype(BF16), order, preferred_element_type=F32)
    rows = rows.astype(jnp.int32)
    paired = jnp.concatenate(halves(h), 1)
    slots = lax.broadcasted_iota(jnp.int32, (R, DEVICES), 0)
    for c in range(CAP):
        line = lax.broadcast_in_dim(rows[c : c + 1], (R, DEVICES), (0, 1))
        hot = jnp.where(slots == line, 1.0, 0.0).astype(BF16)
        got = fold(
            lax.dot_general(hot, paired, (((0,), (0,)), ((), ())), preferred_element_type=F32)
        )
        keep[c * CHIPS : (c + 1) * CHIPS] = got[:CHIPS]
        send[c * CHIPS : (c + 1) * CHIPS] = got[CHIPS:]


def tail_pack(flags, rows_keep, rows_got, g_keep, g_got, out):
    even = flags[3] == 0
    for q in range(CAP):
        at = slice(q * CHIPS, (q + 1) * CHIPS)
        out[:, q * D : (q + 1) * D] = jnp.where(even, rows_keep[at], rows_got[at])
        out[:, (CAP + q) * D : (CAP + q + 1) * D] = jnp.where(even, rows_got[at], rows_keep[at])
    for q in range(PIECE):
        at = slice(q * CHIPS, (q + 1) * CHIPS)
        out[:, (2 * CAP + q) * D : (2 * CAP + q + 1) * D] = g_keep[at] + g_got[at]


def tail_sum(arrived, out):
    total = jnp.sum(arrived[:, 2 * CAP * D :], axis=0, keepdims=True)
    out[...] = lax.broadcast_in_dim(total, (CHIPS, PIECE * D), (0, 1))


def tail_split(flags, own, other, o_send, o_recv, o_edge, o_node, o_update, rows, sems):
    mine = flags[3]
    for q in range(PIECE):
        at = slice(q * CHIPS, (q + 1) * CHIPS)
        rows[mine, at] = own[:, q * D : (q + 1) * D]
        rows[1 - mine, at] = other[:, q * D : (q + 1) * D]
    copies = []
    for out, at, size in (
        (o_send, 0, D),
        (o_recv, D, D),
        (o_edge, 2 * D, D),
        (o_node, 3 * D, 2 * D),
        (o_update, 5 * D, D),
    ):
        copies.append(
            pltpu.make_async_copy(rows.at[:, at : at + size], out, sems.at[len(copies)])
        )
        copies[-1].start()
    for copy in copies:
        copy.wait()


def vmem(*shape):
    return pltpu.VMEM(shape, F32)


def call(kernel, outs, scratch, args):
    places = {"s": pltpu.SMEM, "v": pltpu.VMEM, "w": pltpu.VMEM, "h": pltpu.HBM}
    return pl.pallas_call(
        kernel,
        out_shape=[
            {"h": pltpu.HBM, "w": pltpu.VMEM, "v": jax.ShapeDtypeStruct}[p](shape, *(kind or (F32,)))
            for p, shape, *kind in outs
        ],
        in_specs=[pl.BlockSpec(memory_space=places[p]) for p, _ in args],
        out_specs=[pl.BlockSpec(memory_space=places[p]) for p, *_ in outs],
        scratch_shapes=scratch,
        compiler_params=pltpu.CompilerParams(vmem_limit_bytes=VMEM_BYTES),
    )(
        *[
            pltpu.with_memory_space_constraint(a, places[p]) if p in "hw" else a
            for p, a in args
        ]
    )


def swap(a, axis, second):
    n = lax.axis_size(axis)
    if second:
        pairs = [(i, (i + 1) % n if i % 2 else (i - 1) % n) for i in range(n)]
    else:
        pairs = [(i, i ^ 1) for i in range(n)]
    return lax.ppermute(a, axis, pairs)


def neighbours_along_gx(own):
    return swap(own, "gx", False), swap(own, "gx", True)


def neighbours_along_gy(first, own, second):
    column = jnp.stack([first, own, second])
    return swap(column, "gy", False), column, swap(column, "gy", True)


def columns(pa, po, pb):
    ra = swap(pa, "gy", False)
    rb = swap(pb, "gy", True)
    return po[0] + ra[0] + rb[0], po[1] + ra[1] + rb[1], po[2] + ra[2] + rb[2]


def collect(pa, po, pb):
    low, mid, high = columns(pa, po, pb)
    return swap(low, "gx", False), mid, swap(high, "gx", True)


def exchange(a):
    groups = [[2 * chip + core for chip in range(CHIPS)] for core in range(2)]
    return lax.all_to_all(
        a, AXES, split_axis=0, concat_axis=0, tiled=True, axis_index_groups=groups
    )


def body(
    initial_latents,
    final_cotangent,
    bin_counts,
    neighbours,
    leave_rows,
    leave_counts,
    w_send,
    w_receive,
    w_edge,
    w_node,
    w_update,
):
    gx, gy = lax.axis_index("gx"), lax.axis_index("gy")
    count = bin_counts[0, 0]
    core = gy % 2
    flags = jnp.stack(
        [
            count,
            ((gx > 0) & (gx < GX - 1)).astype(jnp.int32),
            ((gy > 0) & (gy < GY - 1)).astype(jnp.int32),
            core,
            gx % 2,
        ]
    )
    raw = neighbours[0, 0].T
    h0 = initial_latents[0, 0]
    slots = lax.broadcasted_iota(jnp.int32, (R, D), 0)
    masked = jnp.where(slots < count, h0, FLAG)
    row, table3, big, bins9 = (R, D), (3, R, D), (K, R, D), (BLOCKS, R, D)
    two, rows6, pairs = (2, R, D), (6 * D, D), (2, 6, 2 * D, 2 * D)
    table = pltpu.VMEM((BLOCKS * R, 2 * D), BF16)
    terms = pltpu.VMEM((K * R, 2 * D), BF16)
    dma = pltpu.SemaphoreType.DMA
    w, wt, idx, idxt, h0, cot = call(
        prepare,
        [
            ("w", pairs, BF16), ("w", pairs, BF16), ("w", (R, R), jnp.int32), ("w", (K, R), jnp.int32),
            ("w", row), ("w", row),
        ],
        [vmem(2, 6 * D, D), dma((7,))],
        [
            ("s", flags), ("v", raw),
            ("h", w_send), ("h", w_receive), ("h", w_edge), ("h", w_node), ("h", w_update),
            ("h", h0), ("h", final_cotangent[0, 0]),
        ],
    )
    first, second = neighbours_along_gx(masked)
    first, second, w, wt = lax.optimization_barrier((first, second, w, wt))
    ta, to, tb = neighbours_along_gy(first, masked, second)
    send1, saved, slope0, bins0 = call(
        forward_0,
        [("v", row), ("w", (8, R, D)), ("w", big), ("w", bins9)],
        [table],
        [("s", flags), ("v", ta), ("v", to), ("v", tb), ("w", idx), ("w", h0), ("w", w)],
    )
    first, second = neighbours_along_gx(send1)
    ta, to, tb = neighbours_along_gy(first, send1, second)
    leave = (CHIPS * CAP, D)
    pa, pb, po, h2, rows_keep, rows_send, g1 = call(
        middle_1,
        [
            ("v", table3), ("v", table3), ("v", table3), ("h", row), ("w", leave), ("w", leave), ("w", rows6),
        ],
        [table, vmem(*big), terms, vmem(*row), dma],
        [
            ("s", flags), ("v", ta), ("v", to), ("v", tb), ("w", idx), ("w", idxt), ("w", saved), ("w", cot),
            ("w", w), ("w", wt), ("v", leave_rows[0, 0].T), ("v", leave_counts[0]),
        ],
    )
    rows_got = swap(rows_send, "gy", False)
    ma, mo, mb = collect(pa, po, pb)
    ma, rows_got = lax.optimization_barrier((ma, rows_got))
    pa, pb, po, g_keep, g_send = call(
        backward_0,
        [("w", table3), ("w", table3), ("w", table3), ("w", rows6), ("w", rows6)],
        [terms, vmem(2, 6 * D, D), vmem(*big), vmem(*bins9), dma((2,))],
        [
            ("s", flags), ("w", idxt), ("v", ma), ("v", mo), ("v", mb), ("w", saved), ("h", slope0), ("h", bins0),
            ("w", h0), ("w", g1), ("w", wt),
        ],
    )
    g_got = swap(g_send, "gy", False)
    low, mid, high = columns(pa, po, pb)
    (outgoing,) = call(
        tail_pack,
        [("v", (CHIPS, (2 * CAP + PIECE) * D))],
        [],
        [("s", flags), ("v", rows_keep), ("v", rows_got), ("v", g_keep), ("v", g_got)],
    )
    arrived = exchange(outgoing)
    (pieces,) = call(tail_sum, [("v", (CHIPS, PIECE * D))], [], [("v", arrived)])
    pieces, low, high = lax.optimization_barrier((pieces, low, high))
    own = exchange(pieces)
    grad_initial = swap(low, "gx", False) + mid + swap(high, "gx", True)
    arrivals = arrived[:, : 2 * CAP * D].reshape(DEVICES, CAP, D)
    own, grad_initial, arrivals = lax.optimization_barrier((own, grad_initial, arrivals))
    partner = swap(own, "gy", False)
    sums = call(
        tail_split,
        [("h", two), ("h", two), ("h", two), ("h", (2, 2 * D, D)), ("h", two)],
        [vmem(2, 6 * D, D), dma((5,))],
        [("s", flags), ("v", own), ("v", partner)],
    )
    return (
        h2.reshape(1, 1, R, D),
        arrivals.reshape(1, 1, DEVICES, CAP, D),
        grad_initial.reshape(1, 1, R, D),
        *sums,
    )


def solution(mesh):
    in_specs = (
        P("gx", "gy", None, None),
        P("gx", "gy", None, None),
        P("gx", "gy"),
        P("gx", "gy", None, None),
        P("gx", "gy", None, None),
        P("gx", "gy", None),
        P(),
        P(),
        P(),
        P(),
        P(),
    )
    out_specs = (
        P("gx", "gy", None, None),
        P("gx", "gy", None, None, None),
        P("gx", "gy", None, None),
        P(),
        P(),
        P(),
        P(),
        P(),
    )
    return jax.shard_map(body, mesh=mesh, in_specs=in_specs, out_specs=out_specs, check_vma=False)
```

```python
import jax
import jax.numpy as jnp
from jax import lax
from jax.experimental import pallas as pl
from jax.experimental.pallas import tpu as pltpu
from jax.sharding import PartitionSpec as P

EPS = 1e-05
AXES = ("gx", "gy")
GX, GY = 16, 8
DEVICES = GX * GY
CHIPS = DEVICES // 2
D = 128
R = 128
K = 24
BLOCKS = 9
CAP = 8
PIECE = 6 * D // CHIPS
EACH = 2 * CAP + PIECE
SEND, RECV, EDGE, NODE, UPDATE, EDGE_NODE = 0, 1, 2, 3, 5, 6
FLAG = 1e30
NEVER = -1e30
VMEM_BYTES = 12 * 1024 * 1024
F32, BF16 = jnp.float32, jnp.bfloat16


def halves(a):
    high = a.astype(BF16)
    return high, (a - high.astype(F32)).astype(BF16)


def fold(wide):
    n = wide.shape[1] // 2
    return wide[:, :n] + wide[:, n:]


def pair(b):
    bh, bl = halves(b)
    both = jnp.concatenate([bh, bl], 1)
    return jnp.concatenate([both, both], 0)


def mm(a, paired):
    return fold(jnp.dot(jnp.concatenate(halves(a), 1), paired, preferred_element_type=F32))


def mm_tn(a, b):
    return fold(
        lax.dot_general(
            jnp.concatenate(halves(a), 0),
            pair(b),
            (((0,), (0,)), ((), ())),
            preferred_element_type=F32,
        )
    )


def sigmoid(v):
    return 0.5 + 0.5 * jnp.tanh(0.5 * v)


def silu_and_slope(v):
    s = sigmoid(v)
    t = v * s
    return t, s + t * (1.0 - s)


def block_limits(flags):
    return [
        [
            jnp.where(((xs < 2) | (flags[0] > 0)) & ((ys < 2) | (flags[1] > 0)), 1e20, -1e20)
            for xs in range(3)
        ]
        for ys in range(3)
    ]


def hot_rows(idx, k, blocks):
    lanes = lax.broadcasted_iota(jnp.int32, (R, R), 1)
    return jnp.concatenate(
        [jnp.where(idx[k] == lanes + b * R, 1.0, 0.0).astype(BF16) for b in blocks], 1
    )


def hot_columns(idxt, k, first, count):
    line = lax.broadcast_in_dim(idxt[k : k + 1, :], (count, R), (0, 1))
    rows = lax.broadcasted_iota(jnp.int32, (count, R), 0) + first
    return jnp.where(line == rows, 1.0, 0.0).astype(BF16)


COLUMN, SIDES = (3, 4, 5), (0, 1, 2, 6, 7, 8)


def edge_gather(idx, table, blocks, start, wide):
    hot = jnp.concatenate([hot_rows(idx, start + j, blocks) for j in range(wide)], 0)
    return fold(jnp.dot(hot, table[...], preferred_element_type=F32))


def edge_column(idx, table, receiver, part):
    for start in range(0, K, 8):
        got = edge_gather(idx, table, COLUMN, start, 8)
        for j in range(8):
            part[start + j] = got[j * R : (j + 1) * R] + receiver


def edge_forward(idx, table, part, slope_ref, start, wide, total):
    got = edge_gather(idx, table, SIDES, start, wide)
    for j in range(wide):
        t, slope = silu_and_slope(got[j * R : (j + 1) * R] + part[start + j])
        total = total + t
        slope_ref[start + j] = slope
    return total


def edge_terms(slope_ref, back, terms_ref):
    total = jnp.zeros((R, D), F32)
    for k in range(K):
        d = back * slope_ref[k]
        total = total + d
        high, low = halves(d)
        terms_ref[k * R : (k + 1) * R, 0:D] = high
        terms_ref[k * R : (k + 1) * R, D : 2 * D] = low
    return total


def edge_scatter(idxt, terms_ref, first, count):
    hot = jnp.concatenate([hot_columns(idxt, k, first * R, count * R) for k in range(K)], 1)
    return fold(jnp.dot(hot, terms_ref[...], preferred_element_type=F32))


def node_forward(h, hidden, live, w, step):
    a = mm(h, w[step, NODE]) + mm(hidden, w[step, EDGE_NODE])
    inner, slope = silu_and_slope(a)
    u = mm(inner, w[step, UPDATE])
    c = u - jnp.mean(u, axis=1, keepdims=True)
    scale = lax.rsqrt(jnp.mean(c * c, axis=1, keepdims=True) + EPS)
    n = c * scale
    return h + live * n, inner, slope, n, scale


def node_backward(dh, live, slope, n, scale, wt, step):
    dn = live * dh
    du = scale * (
        dn - jnp.mean(dn, axis=1, keepdims=True) - n * jnp.mean(dn * n, axis=1, keepdims=True)
    )
    da = mm(du, wt[step, UPDATE]) * slope
    back = mm(da, wt[step, EDGE_NODE])
    return du, da, back, dh + mm(da, wt[step, NODE])


def weight_grads(h, hidden, message, inner, du, da, dmessage, drecv):
    return (
        mm_tn(h, drecv),
        mm_tn(hidden, dmessage),
        mm_tn(h, da),
        mm_tn(message, da),
        mm_tn(inner, du),
    )


def mask_dead(counts, h_in, masked, h, live, count, sems):
    copies = [
        pltpu.make_async_copy(counts, count, sems.at[0]),
        pltpu.make_async_copy(h_in, h, sems.at[1]),
    ]
    for copy in copies:
        copy.start()
    for copy in copies:
        copy.wait()
    rows = lax.broadcasted_iota(jnp.int32, (R, D), 0)
    masked[...] = jnp.where(rows < count[0, 0], h[...], FLAG)
    live[...] = jnp.where(rows < count[0, 0], 1.0, 0.0)


def prepare(
    flags, raw_in, send, recv, edge, node, update, cot,
    w, wt, idx, idxt, cot_out,
    f, raw, sems,
):
    copies = [
        pltpu.make_async_copy(src, dst, sems.at[i])
        for i, (src, dst) in enumerate(
            (
                (send, f.at[:, 0:D]),
                (recv, f.at[:, D : 2 * D]),
                (edge, f.at[:, 2 * D : 3 * D]),
                (node, f.at[:, 3 * D : 5 * D]),
                (update, f.at[:, 5 * D : 6 * D]),
                (cot, cot_out),
                (raw_in, raw),
            )
        )
    ]
    for copy in copies:
        copy.start()
    copies.pop().wait()
    place = raw[...] // R
    px = (place >= 3).astype(jnp.int32) + (place >= 6).astype(jnp.int32)
    py = place - 3 * px
    xs = jnp.where(flags[3] == 0, 2 - px, px)
    ys = jnp.where(flags[2] == 0, 2 - py, py)
    slot = (ys * 3 + xs) * R + raw[...] - place * R
    idxt[...] = slot
    tall = jnp.concatenate([slot.astype(F32), jnp.zeros((R - K, R), F32)], 0)
    tall = tall.T.astype(jnp.int32)
    for k in range(K):
        idx[k] = lax.broadcast_in_dim(tall[:, k : k + 1], (R, R), (0, 1))
    for copy in copies:
        copy.wait()
    for step in range(2):
        for m in range(6):
            v = f[step, m * D : (m + 1) * D]
            w[step, m] = pair(v)
            wt[step, m] = pair(v.T)
        both = mm(f[step, 2 * D : 3 * D], w[step, NODE + 1])
        w[step, EDGE_NODE] = pair(both)
        wt[step, EDGE_NODE] = pair(both.T)


def fill(table, at, sent):
    high, low = halves(sent)
    table[at * R : (at + 1) * R, 0:D] = high
    table[at * R : (at + 1) * R, D : 2 * D] = low


def column_0(flags, to, idx, h, w, part, bins_out, table, bins, sem):
    limits = block_limits(flags)[1]
    for xs in range(3):
        keep = to[xs] < limits[xs]
        bins[xs] = jnp.where(keep, to[xs], 0.0)
    copy = pltpu.make_async_copy(bins, bins_out, sem)
    copy.start()
    for xs in range(3):
        keep = to[xs] < limits[xs]
        fill(table, xs, jnp.where(keep, mm(bins[xs], w[0, SEND]), NEVER))
    edge_column(idx, table, mm(h[...], w[0, RECV]), part)
    copy.wait()


def forward_0(
    flags, ta, tb, idx, part, h, live_in, w,
    send_out, saved, slope_out, bins_out,
    table, slope, bins, sems,
):
    limits = block_limits(flags)
    for side, (ref, row) in enumerate(((ta, limits[0]), (tb, limits[2]))):
        for xs in range(3):
            keep = ref[xs] < row[xs]
            b = jnp.where(keep, ref[xs], 0.0)
            bins[side * 3 + xs] = b
            fill(table, side * 3 + xs, jnp.where(keep, mm(b, w[0, SEND]), NEVER))
    copies = [pltpu.make_async_copy(bins, bins_out, sems.at[0])]
    copies[0].start()
    h0, live = h[...], live_in[...]
    hidden = jnp.zeros((R, D), F32)
    for start in range(0, K, 8):
        hidden = edge_forward(idx, table, part, slope, start, 8, hidden)
        some = pl.ds(start, 8)
        copies.append(
            pltpu.make_async_copy(slope.at[some], slope_out.at[some], sems.at[len(copies)])
        )
        copies[-1].start()
    h1, inner, islope, n, scale = node_forward(h0, hidden, live, w, 0)
    send_out[...] = jnp.where(live > 0, mm(h1, w[1, SEND]), NEVER)
    saved[0] = h1
    saved[1] = mm(h1, w[1, RECV])
    saved[2] = hidden
    saved[3] = mm(hidden, w[0, EDGE])
    saved[4] = inner
    saved[5] = islope
    saved[6] = n
    saved[7] = lax.broadcast_in_dim(scale, (R, D), (0, 1))
    for copy in copies:
        copy.wait()


def column_1(flags, to, idx, saved, part, table):
    limits = block_limits(flags)[1]
    for xs in range(3):
        fill(table, xs, jnp.where(limits[xs] > 0, to[xs], NEVER))
    edge_column(idx, table, saved[1], part)


def middle_1(
    flags, ta, tb, idx, idxt, part, saved, cot, live_in, w, wt,
    pa, pb, terms, kept,
    table, slope,
):
    limits = block_limits(flags)
    for side, (ref, row) in enumerate(((ta, limits[0]), (tb, limits[2]))):
        for xs in range(3):
            fill(table, side * 3 + xs, jnp.where(row[xs] > 0, ref[xs], NEVER))
    hidden = lax.fori_loop(
        0,
        2,
        lambda i, total: edge_forward(idx, table, part, slope, i * 12, 12, total),
        jnp.zeros((R, D), F32),
    )
    h1, live = saved[0], live_in[...]
    new, inner, islope, n, scale = node_forward(h1, hidden, live, w, 1)
    du, da, back, dh1 = node_backward(cot[...], live, islope, n, scale, wt, 1)
    drecv = edge_terms(slope, back, terms)
    pa[...] = edge_scatter(idxt, terms, 0, 3).reshape(3, R, D)
    pb[...] = edge_scatter(idxt, terms, 6, 3).reshape(3, R, D)
    for i, value in enumerate((hidden, inner, du, da, drecv, dh1, new)):
        kept[i] = value


def middle_1_rest(
    flags, idxt, terms, kept, saved, w, wt, leave_rows, leave_counts,
    po, h_out, rows_keep, rows_send, g,
    h2, sem,
):
    hidden, inner, du, da, drecv, dh1, new = (kept[i] for i in range(7))
    h2[...] = new
    copy = pltpu.make_async_copy(h2, h_out, sem)
    copy.start()
    pack_leaving(flags, leave_rows, leave_counts, new, rows_keep, rows_send)
    po[...] = edge_scatter(idxt, terms, 3, 3).reshape(3, R, D)
    message = mm(hidden, w[1, EDGE])
    dmessage = mm(da, wt[1, NODE + 1])
    grads = weight_grads(saved[0], hidden, message, inner, du, da, dmessage, drecv)
    for i, value in enumerate(grads):
        g[i * D : (i + 1) * D] = value
    g[5 * D :] = dh1 + mm(drecv, wt[1, RECV])
    copy.wait()


def backward_0(
    idxt, ma, mo, mb, saved, slope_in, column_in, sides_in, g1, live, wt,
    pa, pb, po, sums, terms_out, bins,
    terms, slope, sems,
):
    copies = [
        pltpu.make_async_copy(src, dst, sems.at[i])
        for i, (src, dst) in enumerate(
            (
                (slope_in, slope),
                (sides_in.at[0:3], bins.at[0:3]),
                (column_in, bins.at[3:6]),
                (sides_in.at[3:6], bins.at[6:9]),
            )
        )
    ]
    for copy in copies:
        copy.start()
    dsend = ma[...] + mo[...] + mb[...]
    dh1 = g1[5 * D :] + mm(dsend, wt[1, SEND])
    du, da, back, dh0 = node_backward(dh1, live[...], saved[5], saved[6], saved[7][:, 0:1], wt, 0)
    copies[0].wait()
    drecv = edge_terms(slope, back, terms)
    got = edge_scatter(idxt, terms, 0, BLOCKS)
    for part, out in enumerate((pa, po, pb)):
        for xs in range(3):
            v = got[(part * 3 + xs) * R : (part * 3 + xs + 1) * R]
            sums[part * 3 + xs] = v
            out[xs] = mm(v, wt[0, SEND])
    po[1] += dh0 + mm(drecv, wt[0, RECV])
    terms_out[0] = du
    terms_out[1] = da
    terms_out[2] = drecv
    terms_out[3] = dsend
    for copy in copies[1:]:
        copy.wait()


def grads_0(flags, saved, bins, sums, parts, h, g1, wt, keep, send, g):
    du, da, drecv, dsend = (parts[i] for i in range(4))
    dmessage = mm(da, wt[0, NODE + 1])
    total = mm_tn(bins[0], sums[0])
    for b in range(1, BLOCKS):
        total = total + mm_tn(bins[b], sums[b])
    g[0, 0:D] = total
    grads = weight_grads(h[...], saved[2], saved[3], saved[4], du, da, dmessage, drecv)
    for i, value in enumerate(grads):
        g[0, (i + 1) * D : (i + 2) * D] = value
    g[1, 0:D] = mm_tn(saved[0], dsend)
    g[1, D:] = g1[0 : 5 * D]
    mine = flags[2]
    keep[...] = g[mine]
    send[...] = g[1 - mine]


def pack_leaving(flags, rows, counts, h, keep, send):
    q = lax.broadcasted_iota(jnp.int32, (CAP, DEVICES), 0)
    rows = jnp.where(q < lax.broadcast_in_dim(counts[...], (CAP, DEVICES), (0, 1)), rows[...], -1)
    target = lax.broadcasted_iota(jnp.int32, (DEVICES, DEVICES), 0)
    at = lax.broadcasted_iota(jnp.int32, (DEVICES, DEVICES), 1)
    first = at < CHIPS
    wanted = jnp.where(first, 2 * at + flags[2], 2 * (at - CHIPS) + 1 - flags[2])
    order = jnp.where(target == wanted, 1.0, 0.0).astype(BF16)
    rows = jnp.dot(rows.astype(F32).astype(BF16), order, preferred_element_type=F32)
    rows = rows.astype(jnp.int32)
    paired = jnp.concatenate(halves(h), 1)
    slots = lax.broadcasted_iota(jnp.int32, (R, DEVICES), 0)
    for c in range(CAP):
        line = lax.broadcast_in_dim(rows[c : c + 1], (R, DEVICES), (0, 1))
        hot = jnp.where(slots == line, 1.0, 0.0).astype(BF16)
        got = fold(
            lax.dot_general(hot, paired, (((0,), (0,)), ((), ())), preferred_element_type=F32)
        )
        keep[c * CHIPS : (c + 1) * CHIPS] = got[:CHIPS]
        send[c * CHIPS : (c + 1) * CHIPS] = got[CHIPS:]


def tail_pack(flags, rows_keep, rows_got, g_keep, g_got, out):
    even = flags[2] == 0
    for q in range(CAP):
        at = slice(q * CHIPS, (q + 1) * CHIPS)
        out[pl.ds(q, CHIPS, stride=EACH)] = jnp.where(even, rows_keep[at], rows_got[at])
        out[pl.ds(CAP + q, CHIPS, stride=EACH)] = jnp.where(even, rows_got[at], rows_keep[at])
    for i in range(CHIPS):
        at = slice(i * PIECE, (i + 1) * PIECE)
        out[i * EACH + 2 * CAP : (i + 1) * EACH] = g_keep[at] + g_got[at]


def tail_sum(arrived, out):
    for q in range(PIECE):
        rows = arrived[pl.ds(2 * CAP + q, CHIPS, stride=EACH)]
        total = jnp.sum(rows, axis=0, keepdims=True)
        out[pl.ds(q, CHIPS, stride=PIECE)] = lax.broadcast_in_dim(total, (CHIPS, D), (0, 1))


def take_arrivals(arrived, out, rows, sem):
    for i in range(CHIPS):
        rows[i * 2 * CAP : (i + 1) * 2 * CAP] = arrived[i * EACH : i * EACH + 2 * CAP]
    copy = pltpu.make_async_copy(rows, out, sem)
    copy.start()
    copy.wait()


def tail_split(flags, own, other, o_send, o_recv, o_edge, o_node, o_update, sems):
    mine = flags[2]
    copies = []
    for out, at, size in (
        (o_send, 0, D),
        (o_recv, D, D),
        (o_edge, 2 * D, D),
        (o_node, 3 * D, 2 * D),
        (o_update, 5 * D, D),
    ):
        for rows, step in ((own, mine), (other, 1 - mine)):
            copies.append(
                pltpu.make_async_copy(rows.at[at : at + size], out.at[step], sems.at[len(copies)])
            )
            copies[-1].start()
    for copy in copies:
        copy.wait()


def vmem(*shape):
    return pltpu.VMEM(shape, F32)


def call(kernel, outs, scratch, args, microseconds=1.0):
    places = {"s": pltpu.SMEM, "v": pltpu.VMEM, "w": pltpu.VMEM, "h": pltpu.HBM, "a": pl.ANY}
    return pl.pallas_call(
        kernel,
        out_shape=[
            {"h": pltpu.HBM, "w": pltpu.VMEM, "v": jax.ShapeDtypeStruct}[p](shape, *(kind or (F32,)))
            for p, shape, *kind in outs
        ],
        in_specs=[pl.BlockSpec(memory_space=places[p]) for p, _ in args],
        out_specs=[pl.BlockSpec(memory_space=places[p]) for p, *_ in outs],
        scratch_shapes=scratch,
        compiler_params=pltpu.CompilerParams(vmem_limit_bytes=VMEM_BYTES),
        cost_estimate=pl.CostEstimate(
            flops=int(microseconds * 1e9), bytes_accessed=int(microseconds * 3e6), transcendentals=0
        ),
    )(
        *[
            pltpu.with_memory_space_constraint(a, places[p]) if p in "hw" else a
            for p, a in args
        ]
    )


def swap(a, axis, second):
    n = lax.axis_size(axis)
    if second:
        pairs = [(i, (i + 1) % n if i % 2 else (i - 1) % n) for i in range(n)]
    else:
        pairs = [(i, i ^ 1) for i in range(n)]
    return lax.ppermute(a, axis, pairs)


def neighbours_along_gx(own):
    return swap(own, "gx", False), swap(own, "gx", True)


def neighbours_along_gy(first, own, second):
    column = jnp.stack([first, own, second])
    return swap(column, "gy", False), column, swap(column, "gy", True)


def along_gy(pa, pb):
    return swap(pa, "gy", False), swap(pb, "gy", True)


def columns(ra, po, rb):
    return po[0] + ra[0] + rb[0], po[1] + ra[1] + rb[1], po[2] + ra[2] + rb[2]


def exchange(a):
    groups = [[2 * chip + core for chip in range(CHIPS)] for core in range(2)]
    moved = lax.all_to_all(
        a.reshape(CHIPS, 1, -1),
        AXES,
        split_axis=0,
        concat_axis=0,
        tiled=True,
        axis_index_groups=groups,
    )
    return moved.reshape(a.shape)


def body(
    initial_latents,
    final_cotangent,
    bin_counts,
    neighbours,
    leave_rows,
    leave_counts,
    w_send,
    w_receive,
    w_edge,
    w_node,
    w_update,
):
    gx, gy = lax.axis_index("gx"), lax.axis_index("gy")
    core = gy % 2
    flags = jnp.stack(
        [
            ((gx > 0) & (gx < GX - 1)).astype(jnp.int32),
            ((gy > 0) & (gy < GY - 1)).astype(jnp.int32),
            core,
            gx % 2,
        ]
    )
    raw = neighbours[0, 0].T
    row, table3, big, bins9 = (R, D), (3, R, D), (K, R, D), (BLOCKS, R, D)
    two, rows6, pairs = (2, R, D), (6 * D, D), (2, 7, 2 * D, 2 * D)
    terms = pltpu.VMEM((K * R, 2 * D), BF16)
    dma = pltpu.SemaphoreType.DMA
    masked, h0, live = call(
        mask_dead,
        [("v", row), ("w", row), ("w", row)],
        [pltpu.SMEM((1, 1), jnp.int32), dma((2,))],
        [("a", bin_counts), ("h", initial_latents[0, 0])],
    )
    first, second = neighbours_along_gx(masked)
    w, wt, idx, idxt, cot = call(
        prepare,
        [
            ("w", pairs, BF16), ("w", pairs, BF16), ("w", big, jnp.int32), ("w", (K, R), jnp.int32),
            ("w", row),
        ],
        [vmem(2, 6 * D, D), pltpu.VMEM((K, R), jnp.int32), dma((7,))],
        [
            ("s", flags), ("h", raw),
            ("h", w_send), ("h", w_receive), ("h", w_edge), ("h", w_node), ("h", w_update),
            ("h", final_cotangent[0, 0]),
        ],
    )
    first, second, w, idx = lax.optimization_barrier((first, second, w, idx))
    ta, to, tb = neighbours_along_gy(first, masked, second)
    half = pltpu.VMEM((3 * R, 2 * D), BF16)
    sides = pltpu.VMEM((6 * R, 2 * D), BF16)
    bins6 = (6, R, D)
    part, column_bins = call(
        column_0,
        [("w", big), ("h", table3)],
        [half, vmem(*table3), dma],
        [("s", flags), ("v", to), ("w", idx), ("w", h0), ("w", w)],
    )
    send1, saved, slope0, side_bins = call(
        forward_0,
        [("v", row), ("w", (8, R, D)), ("h", big), ("h", bins6)],
        [sides, vmem(*big), vmem(*bins6), dma((4,))],
        [("s", flags), ("v", ta), ("v", tb), ("w", idx), ("w", part), ("w", h0), ("w", live), ("w", w)],
    )
    first, second = neighbours_along_gx(send1)
    ta, to, tb = neighbours_along_gy(first, send1, second)
    (part,) = call(
        column_1, [("w", big)], [half], [("s", flags), ("v", to), ("w", idx), ("w", saved)]
    )
    pa, pb, terms1, kept = call(
        middle_1,
        [("v", table3), ("v", table3), ("w", (K * R, 2 * D), BF16), ("w", (7, R, D))],
        [sides, vmem(*big)],
        [
            ("s", flags), ("v", ta), ("v", tb), ("w", idx), ("w", idxt), ("w", part), ("w", saved), ("w", cot),
            ("w", live), ("w", w), ("w", wt),
        ],
    )
    ra, rb = along_gy(pa, pb)
    leave = (CHIPS * CAP, D)
    po, h2, rows_keep, rows_send, g1 = call(
        middle_1_rest,
        [("v", table3), ("h", row), ("w", leave), ("w", leave), ("w", rows6)],
        [vmem(*row), dma],
        [
            ("s", flags), ("w", idxt), ("w", terms1), ("w", kept), ("w", saved), ("w", w), ("w", wt),
            ("v", leave_rows[0, 0].T), ("v", leave_counts[0]),
        ],
    )
    rows_got = swap(rows_send, "gy", False)
    low, mo, high = columns(ra, po, rb)
    mb = swap(high, "gx", True)
    ma = swap(low, "gx", False)
    ma, mb, rows_got = lax.optimization_barrier((ma, mb, rows_got))
    pa, pb, po, sums0, parts0, bins0 = call(
        backward_0,
        [("w", table3), ("w", table3), ("w", table3), ("w", bins9), ("w", (4, R, D)), ("w", bins9)],
        [terms, vmem(*big), dma((4,))],
        [
            ("w", idxt), ("v", ma), ("v", mo), ("v", mb), ("w", saved), ("h", slope0),
            ("h", column_bins), ("h", side_bins), ("w", g1), ("w", live), ("w", wt),
        ],
    )
    g_keep, g_send = call(
        grads_0,
        [("w", rows6), ("w", rows6)],
        [vmem(2, 6 * D, D)],
        [
            ("s", flags), ("w", saved), ("w", bins0), ("w", sums0), ("w", parts0), ("w", h0), ("w", g1), ("w", wt),
        ],
        5.0,
    )
    g_got = swap(g_send, "gy", False)
    ra, rb = along_gy(pa, pb)
    (outgoing,) = call(
        tail_pack,
        [("v", (CHIPS * EACH, D))],
        [],
        [("s", flags), ("v", rows_keep), ("v", rows_got), ("v", g_keep), ("v", g_got)],
        0.01,
    )
    outgoing, ra, rb = lax.optimization_barrier((outgoing, ra, rb))
    arrived = exchange(outgoing)
    (pieces,) = call(tail_sum, [("v", (CHIPS * PIECE, D))], [], [("v", arrived)])
    own = exchange(pieces)
    low, mid, high = columns(ra, po, rb)
    second = swap(high, "gx", True)
    first = swap(low, "gx", False)
    (arrivals,) = call(
        take_arrivals,
        [("h", (DEVICES * CAP, D))],
        [vmem(DEVICES * CAP, D), dma],
        [("v", arrived)],
    )
    own, first, second, arrivals = lax.optimization_barrier((own, first, second, arrivals))
    grad_initial = first + mid + second
    partner = swap(own, "gy", False)
    sums = call(
        tail_split,
        [("h", two), ("h", two), ("h", two), ("h", (2, 2 * D, D)), ("h", two)],
        [dma((10,))],
        [("s", flags), ("v", own), ("v", partner)],
    )
    return (
        h2.reshape(1, 1, R, D),
        arrivals.reshape(1, 1, DEVICES, CAP, D),
        grad_initial.reshape(1, 1, R, D),
        *sums,
    )


def solution(mesh):
    in_specs = (
        P("gx", "gy", None, None),
        P("gx", "gy", None, None),
        P("gx", "gy"),
        P("gx", "gy", None, None),
        P("gx", "gy", None, None),
        P("gx", "gy", None),
        P(),
        P(),
        P(),
        P(),
        P(),
    )
    out_specs = (
        P("gx", "gy", None, None),
        P("gx", "gy", None, None, None),
        P("gx", "gy", None, None),
        P(),
        P(),
        P(),
        P(),
        P(),
    )
    return jax.shard_map(body, mesh=mesh, in_specs=in_specs, out_specs=out_specs, check_vma=False)
```

```python
import jax
import jax.numpy as jnp
from jax import lax
from jax.experimental import pallas as pl
from jax.experimental.pallas import tpu as pltpu
from jax.sharding import PartitionSpec as P

EPS = 1e-05
AXES = ("gx", "gy")
GX, GY = 16, 8
DEVICES = GX * GY
CHIPS = DEVICES // 2
D = 128
R = 128
K = 24
BLOCKS = 9
CAP = 8
PIECE = 6 * D // CHIPS
EACH = 2 * CAP + PIECE
CUTS = (0, 22, 44, CHIPS)
SEND, RECV, EDGE, NODE, UPDATE, EDGE_NODE = 0, 1, 2, 3, 5, 6
FLAG = 1e30
NEVER = -1e30
VMEM_BYTES = 12 * 1024 * 1024
F32, BF16 = jnp.float32, jnp.bfloat16


def halves(a):
    high = a.astype(BF16)
    return high, (a - high.astype(F32)).astype(BF16)


def fold(wide):
    n = wide.shape[1] // 2
    return wide[:, :n] + wide[:, n:]


def pair(b):
    bh, bl = halves(b)
    both = jnp.concatenate([bh, bl], 1)
    return jnp.concatenate([both, both], 0)


def mm(a, paired):
    return fold(jnp.dot(jnp.concatenate(halves(a), 1), paired, preferred_element_type=F32))


def mm_tn(a, b):
    return fold(
        lax.dot_general(
            jnp.concatenate(halves(a), 0),
            pair(b),
            (((0,), (0,)), ((), ())),
            preferred_element_type=F32,
        )
    )


def sigmoid(v):
    return 0.5 + 0.5 * jnp.tanh(0.5 * v)


def silu_and_slope(v):
    s = sigmoid(v)
    t = v * s
    return t, s + t * (1.0 - s)


def block_limits(flags):
    return [
        [
            jnp.where(((xs < 2) | (flags[0] > 0)) & ((ys < 2) | (flags[1] > 0)), 1e20, -1e20)
            for xs in range(3)
        ]
        for ys in range(3)
    ]


def hot_rows(idx, k, blocks):
    lanes = lax.broadcasted_iota(jnp.int32, (R, R), 1)
    return jnp.concatenate(
        [jnp.where(idx[k] == lanes + b * R, 1.0, 0.0).astype(BF16) for b in blocks], 1
    )


def hot_columns(idxt, k, first, count):
    line = lax.broadcast_in_dim(idxt[k : k + 1, :], (count, R), (0, 1))
    rows = lax.broadcasted_iota(jnp.int32, (count, R), 0) + first
    return jnp.where(line == rows, 1.0, 0.0).astype(BF16)


PARTNER, COLUMN, NEXT = (0, 1, 2), (3, 4, 5), (6, 7, 8)


def edge_gather(idx, table, blocks, start, wide):
    hot = jnp.concatenate([hot_rows(idx, start + j, blocks) for j in range(wide)], 0)
    return fold(jnp.dot(hot, table[...], preferred_element_type=F32))


def edge_add(idx, table, blocks, more, part):
    for start in range(0, K, 8):
        got = edge_gather(idx, table, blocks, start, 8)
        for j in range(8):
            part[start + j] = got[j * R : (j + 1) * R] + more(start + j)


def edge_forward(idx, table, part, slope_ref, start, wide, total):
    got = edge_gather(idx, table, NEXT, start, wide)
    for j in range(wide):
        t, slope = silu_and_slope(got[j * R : (j + 1) * R] + part[start + j])
        total = total + t
        slope_ref[start + j] = slope
    return total


def edge_terms(slope_ref, back, terms_ref):
    total = jnp.zeros((R, D), F32)
    for k in range(K):
        d = back * slope_ref[k]
        total = total + d
        high, low = halves(d)
        terms_ref[k * R : (k + 1) * R, 0:D] = high
        terms_ref[k * R : (k + 1) * R, D : 2 * D] = low
    return total


def edge_scatter(idxt, terms_ref, first, count):
    hot = jnp.concatenate([hot_columns(idxt, k, first * R, count * R) for k in range(K)], 1)
    return fold(jnp.dot(hot, terms_ref[...], preferred_element_type=F32))


def node_forward(h, hidden, live, w, step):
    a = mm(h, w[step, NODE]) + mm(hidden, w[step, EDGE_NODE])
    inner, slope = silu_and_slope(a)
    u = mm(inner, w[step, UPDATE])
    c = u - jnp.mean(u, axis=1, keepdims=True)
    scale = lax.rsqrt(jnp.mean(c * c, axis=1, keepdims=True) + EPS)
    n = c * scale
    return h + live * n, inner, slope, n, scale


def node_backward(dh, live, slope, n, scale, wt, step):
    dn = live * dh
    du = scale * (
        dn - jnp.mean(dn, axis=1, keepdims=True) - n * jnp.mean(dn * n, axis=1, keepdims=True)
    )
    da = mm(du, wt[step, UPDATE]) * slope
    back = mm(da, wt[step, EDGE_NODE])
    return du, da, back, dh + mm(da, wt[step, NODE])


def weight_grads(h, hidden, message, inner, du, da, dmessage, drecv):
    return (
        mm_tn(h, drecv),
        mm_tn(hidden, dmessage),
        mm_tn(h, da),
        mm_tn(message, da),
        mm_tn(inner, du),
    )


def mask_dead(counts, h_in, masked, h, live, count, sems):
    copies = [
        pltpu.make_async_copy(counts, count, sems.at[0]),
        pltpu.make_async_copy(h_in, h, sems.at[1]),
    ]
    for copy in copies:
        copy.start()
    for copy in copies:
        copy.wait()
    rows = lax.broadcasted_iota(jnp.int32, (R, D), 0)
    masked[...] = jnp.where(rows < count[0, 0], h[...], FLAG)
    live[...] = jnp.where(rows < count[0, 0], 1.0, 0.0)


def prepare(
    flags, raw_in, send, recv, edge, node, update, cot,
    w, wt, idx, idxt, cot_out,
    f, raw, sems,
):
    copies = [
        pltpu.make_async_copy(src, dst, sems.at[i])
        for i, (src, dst) in enumerate(
            (
                (send, f.at[:, 0:D]),
                (recv, f.at[:, D : 2 * D]),
                (edge, f.at[:, 2 * D : 3 * D]),
                (node, f.at[:, 3 * D : 5 * D]),
                (update, f.at[:, 5 * D : 6 * D]),
                (cot, cot_out),
                (raw_in, raw),
            )
        )
    ]
    for copy in copies:
        copy.start()
    copies.pop().wait()
    place = raw[...] // R
    px = (place >= 3).astype(jnp.int32) + (place >= 6).astype(jnp.int32)
    py = place - 3 * px
    xs = jnp.where(flags[3] == 0, 2 - px, px)
    ys = jnp.where(flags[2] == 0, 2 - py, py)
    slot = (ys * 3 + xs) * R + raw[...] - place * R
    idxt[...] = slot
    tall = jnp.concatenate([slot.astype(F32), jnp.zeros((R - K, R), F32)], 0)
    tall = tall.T.astype(jnp.int32)
    for k in range(K):
        idx[k] = lax.broadcast_in_dim(tall[:, k : k + 1], (R, R), (0, 1))
    for copy in copies:
        copy.wait()
    for step in range(2):
        for m in range(6):
            v = f[step, m * D : (m + 1) * D]
            w[step, m] = pair(v)
            wt[step, m] = pair(v.T)
        both = mm(f[step, 2 * D : 3 * D], w[step, NODE + 1])
        w[step, EDGE_NODE] = pair(both)
        wt[step, EDGE_NODE] = pair(both.T)


def fill(table, at, sent):
    high, low = halves(sent)
    table[at * R : (at + 1) * R, 0:D] = high
    table[at * R : (at + 1) * R, D : 2 * D] = low


def project(refs, limits, w, bins, table):
    for xs in range(3):
        v = refs[xs][...]
        keep = v < limits[xs]
        b = jnp.where(keep, v, 0.0)
        bins[xs] = b
        fill(table, xs, jnp.where(keep, mm(b, w[0, SEND]), NEVER))


def column_0(flags, to, idx, h, w, part, bins, table):
    project([to.at[xs] for xs in range(3)], block_limits(flags)[1], w, bins, table)
    receiver = mm(h[...], w[0, RECV])
    edge_add(idx, table, COLUMN, lambda k: receiver, part)


def partner_0(flags, t0, t1, t2, idx, part_in, w, part, bins, table):
    project((t0, t1, t2), block_limits(flags)[0], w, bins, table)
    edge_add(idx, table, PARTNER, lambda k: part_in[k], part)


def forward_0(
    flags, tb, idx, part, h, live_in, w,
    send_out, slope, bins, kept,
    table,
):
    project([tb.at[xs] for xs in range(3)], block_limits(flags)[2], w, bins, table)
    h0, live = h[...], live_in[...]
    hidden = jnp.zeros((R, D), F32)
    for start in range(0, K, 8):
        hidden = edge_forward(idx, table, part, slope, start, 8, hidden)
    h1, inner, islope, n, scale = node_forward(h0, hidden, live, w, 0)
    send_out[...] = jnp.where(live > 0, mm(h1, w[1, SEND]), NEVER)
    for i, value in enumerate((h1, hidden, inner, islope, n)):
        kept[i] = value
    kept[5] = lax.broadcast_in_dim(scale, (R, D), (0, 1))


def forward_0_rest(kept, slope, partner, column, across, w, slope_out, bins_out, saved, sems):
    copies = [
        pltpu.make_async_copy(slope, slope_out, sems.at[0]),
        pltpu.make_async_copy(partner, bins_out.at[0:3], sems.at[1]),
        pltpu.make_async_copy(column, bins_out.at[3:6], sems.at[2]),
        pltpu.make_async_copy(across, bins_out.at[6:9], sems.at[3]),
    ]
    for copy in copies:
        copy.start()
    saved[0] = kept[0]
    saved[1] = mm(kept[0], w[1, RECV])
    saved[2] = kept[1]
    saved[3] = mm(kept[1], w[0, EDGE])
    for i in range(2, 6):
        saved[i + 2] = kept[i]
    for copy in copies:
        copy.wait()


def mask_sent(refs, limits, table):
    for xs in range(3):
        fill(table, xs, jnp.where(limits[xs] > 0, refs[xs][...], NEVER))


def column_1(flags, to, idx, saved, part, table):
    mask_sent([to.at[xs] for xs in range(3)], block_limits(flags)[1], table)
    edge_add(idx, table, COLUMN, lambda k: saved[1], part)


def partner_1(flags, t0, t1, t2, idx, part_in, part, table):
    mask_sent((t0, t1, t2), block_limits(flags)[0], table)
    edge_add(idx, table, PARTNER, lambda k: part_in[k], part)


def middle_1(
    flags, tb, idx, idxt, part, saved, cot, live_in, w, wt,
    pa, pb, terms, kept,
    table, slope,
):
    mask_sent([tb.at[xs] for xs in range(3)], block_limits(flags)[2], table)
    hidden = jnp.zeros((R, D), F32)
    for start in range(0, K, 8):
        hidden = edge_forward(idx, table, part, slope, start, 8, hidden)
    h1, live = saved[0], live_in[...]
    new, inner, islope, n, scale = node_forward(h1, hidden, live, w, 1)
    du, da, back, dh1 = node_backward(cot[...], live, islope, n, scale, wt, 1)
    drecv = edge_terms(slope, back, terms)
    pa[...] = edge_scatter(idxt, terms, 0, 3).reshape(3, R, D)
    pb[...] = edge_scatter(idxt, terms, 6, 3).reshape(3, R, D)
    for i, value in enumerate((hidden, inner, du, da, drecv, dh1, new)):
        kept[i] = value


def middle_1_rest(
    flags, idxt, terms, kept, saved, w, wt, leave_rows, leave_counts,
    po, h_out, rows_keep, rows_send, g,
    h2, sem,
):
    hidden, inner, du, da, drecv, dh1, new = (kept[i] for i in range(7))
    h2[...] = new
    copy = pltpu.make_async_copy(h2, h_out, sem)
    copy.start()
    pack_leaving(flags, leave_rows, leave_counts, new, rows_keep, rows_send)
    po[...] = edge_scatter(idxt, terms, 3, 3).reshape(3, R, D)
    message = mm(hidden, w[1, EDGE])
    dmessage = mm(da, wt[1, NODE + 1])
    grads = weight_grads(saved[0], hidden, message, inner, du, da, dmessage, drecv)
    for i, value in enumerate(grads):
        g[i * D : (i + 1) * D] = value
    g[5 * D :] = dh1 + mm(drecv, wt[1, RECV])
    copy.wait()


def backward_0(
    idxt, ma, mo, mb, saved, slope_in, bins_in, g1, live, wt,
    pa, pb, po, sums, terms_out, bins,
    terms, slope, sems,
):
    copies = [
        pltpu.make_async_copy(src, dst, sems.at[i])
        for i, (src, dst) in enumerate(
            (
                (slope_in, slope),
                (bins_in, bins),
            )
        )
    ]
    for copy in copies:
        copy.start()
    dsend = ma[...] + mo[...] + mb[...]
    dh1 = g1[5 * D :] + mm(dsend, wt[1, SEND])
    du, da, back, dh0 = node_backward(dh1, live[...], saved[5], saved[6], saved[7][:, 0:1], wt, 0)
    copies[0].wait()
    drecv = edge_terms(slope, back, terms)
    got = edge_scatter(idxt, terms, 0, BLOCKS)
    for part, out in enumerate((pa, po, pb)):
        for xs in range(3):
            v = got[(part * 3 + xs) * R : (part * 3 + xs + 1) * R]
            sums[part * 3 + xs] = v
            out[xs] = mm(v, wt[0, SEND])
    po[1] += dh0 + mm(drecv, wt[0, RECV])
    terms_out[0] = du
    terms_out[1] = da
    terms_out[2] = drecv
    terms_out[3] = dsend
    for copy in copies[1:]:
        copy.wait()


def grads_0(flags, saved, bins, sums, parts, h, g1, wt, keep, *rest):
    *send, g = rest
    du, da, drecv, dsend = (parts[i] for i in range(4))
    dmessage = mm(da, wt[0, NODE + 1])
    total = mm_tn(bins[0], sums[0])
    for b in range(1, BLOCKS):
        total = total + mm_tn(bins[b], sums[b])
    g[0, 0:D] = total
    grads = weight_grads(h[...], saved[2], saved[3], saved[4], du, da, dmessage, drecv)
    for i, value in enumerate(grads):
        g[0, (i + 1) * D : (i + 2) * D] = value
    g[1, 0:D] = mm_tn(saved[0], dsend)
    g[1, D:] = g1[0 : 5 * D]
    mine = flags[2]
    keep[...] = g[mine]
    for out, first, last in zip(send, CUTS, CUTS[1:]):
        out[...] = g[1 - mine, first * PIECE : last * PIECE]


def pack_leaving(flags, rows, counts, h, keep, send):
    q = lax.broadcasted_iota(jnp.int32, (CAP, DEVICES), 0)
    rows = jnp.where(q < lax.broadcast_in_dim(counts[...], (CAP, DEVICES), (0, 1)), rows[...], -1)
    target = lax.broadcasted_iota(jnp.int32, (DEVICES, DEVICES), 0)
    at = lax.broadcasted_iota(jnp.int32, (DEVICES, DEVICES), 1)
    first = at < CHIPS
    wanted = jnp.where(first, 2 * at + flags[2], 2 * (at - CHIPS) + 1 - flags[2])
    order = jnp.where(target == wanted, 1.0, 0.0).astype(BF16)
    rows = jnp.dot(rows.astype(F32).astype(BF16), order, preferred_element_type=F32)
    rows = rows.astype(jnp.int32)
    paired = jnp.concatenate(halves(h), 1)
    slots = lax.broadcasted_iota(jnp.int32, (R, DEVICES), 0)
    for c in range(CAP):
        line = lax.broadcast_in_dim(rows[c : c + 1], (R, DEVICES), (0, 1))
        hot = jnp.where(slots == line, 1.0, 0.0).astype(BF16)
        got = fold(
            lax.dot_general(hot, paired, (((0,), (0,)), ((), ())), preferred_element_type=F32)
        )
        keep[c * CHIPS : (c + 1) * CHIPS] = got[:CHIPS]
        send[c * CHIPS : (c + 1) * CHIPS] = got[CHIPS:]


def tail_pack(flags, rows_keep, rows_got, g_keep, *rest):
    *g_got, out = rest
    even = flags[2] == 0
    for q in range(CAP):
        at = slice(q * CHIPS, (q + 1) * CHIPS)
        out[pl.ds(q, CHIPS, stride=EACH)] = jnp.where(even, rows_keep[at], rows_got[at])
        out[pl.ds(CAP + q, CHIPS, stride=EACH)] = jnp.where(even, rows_got[at], rows_keep[at])
    for got, first, last in zip(g_got, CUTS, CUTS[1:]):
        for i in range(first, last):
            near = got[(i - first) * PIECE : (i - first + 1) * PIECE]
            out[i * EACH + 2 * CAP : (i + 1) * EACH] = g_keep[i * PIECE : (i + 1) * PIECE] + near


def tail_sum(arrived, out):
    for q in range(PIECE):
        rows = arrived[pl.ds(2 * CAP + q, CHIPS, stride=EACH)]
        total = jnp.sum(rows, axis=0, keepdims=True)
        out[pl.ds(q, CHIPS, stride=PIECE)] = lax.broadcast_in_dim(total, (CHIPS, D), (0, 1))


def take_arrivals(arrived, out, rows, sem):
    for i in range(CHIPS):
        rows[i * 2 * CAP : (i + 1) * 2 * CAP] = arrived[i * EACH : i * EACH + 2 * CAP]
    copy = pltpu.make_async_copy(rows, out, sem)
    copy.start()
    copy.wait()


def tail_split(flags, own, other, o_send, o_recv, o_edge, o_node, o_update, sems):
    mine = flags[2]
    copies = []
    for out, at, size in (
        (o_send, 0, D),
        (o_recv, D, D),
        (o_edge, 2 * D, D),
        (o_node, 3 * D, 2 * D),
        (o_update, 5 * D, D),
    ):
        for rows, step in ((own, mine), (other, 1 - mine)):
            copies.append(
                pltpu.make_async_copy(rows.at[at : at + size], out.at[step], sems.at[len(copies)])
            )
            copies[-1].start()
    for copy in copies:
        copy.wait()


def vmem(*shape):
    return pltpu.VMEM(shape, F32)


def call(kernel, outs, scratch, args, microseconds=1.0):
    places = {"s": pltpu.SMEM, "v": pltpu.VMEM, "w": pltpu.VMEM, "h": pltpu.HBM, "a": pl.ANY}
    return pl.pallas_call(
        kernel,
        out_shape=[
            {"h": pltpu.HBM, "w": pltpu.VMEM, "v": jax.ShapeDtypeStruct}[p](shape, *(kind or (F32,)))
            for p, shape, *kind in outs
        ],
        in_specs=[pl.BlockSpec(memory_space=places[p]) for p, _ in args],
        out_specs=[pl.BlockSpec(memory_space=places[p]) for p, *_ in outs],
        scratch_shapes=scratch,
        compiler_params=pltpu.CompilerParams(vmem_limit_bytes=VMEM_BYTES),
        cost_estimate=pl.CostEstimate(
            flops=int(microseconds * 1e9), bytes_accessed=int(microseconds * 3e6), transcendentals=0
        ),
    )(
        *[
            pltpu.with_memory_space_constraint(a, places[p]) if p in "hw" else a
            for p, a in args
        ]
    )


def swap(a, axis, second):
    n = lax.axis_size(axis)
    if second:
        pairs = [(i, (i + 1) % n if i % 2 else (i - 1) % n) for i in range(n)]
    else:
        pairs = [(i, i ^ 1) for i in range(n)]
    return lax.ppermute(a, axis, pairs)


def neighbours_along_gx(own):
    return swap(own, "gx", False), swap(own, "gx", True)


def neighbours_along_gy(first, own, second):
    column = jnp.stack([first, own, second])
    return [swap(a, "gy", False) for a in (first, own, second)], column, swap(column, "gy", True)


def along_gy(pa, pb):
    return swap(pa, "gy", False), swap(pb, "gy", True)


def columns(ra, po, rb):
    return po[0] + ra[0] + rb[0], po[1] + ra[1] + rb[1], po[2] + ra[2] + rb[2]


def exchange(a):
    groups = [[2 * chip + core for chip in range(CHIPS)] for core in range(2)]
    moved = lax.all_to_all(
        a.reshape(CHIPS, 1, -1),
        AXES,
        split_axis=0,
        concat_axis=0,
        tiled=True,
        axis_index_groups=groups,
    )
    return moved.reshape(a.shape)


def body(
    initial_latents,
    final_cotangent,
    bin_counts,
    neighbours,
    leave_rows,
    leave_counts,
    w_send,
    w_receive,
    w_edge,
    w_node,
    w_update,
):
    gx, gy = lax.axis_index("gx"), lax.axis_index("gy")
    core = gy % 2
    flags = jnp.stack(
        [
            ((gx > 0) & (gx < GX - 1)).astype(jnp.int32),
            ((gy > 0) & (gy < GY - 1)).astype(jnp.int32),
            core,
            gx % 2,
        ]
    )
    raw = neighbours[0, 0].T
    row, table3, big, bins9 = (R, D), (3, R, D), (K, R, D), (BLOCKS, R, D)
    two, rows6, pairs = (2, R, D), (6 * D, D), (2, 7, 2 * D, 2 * D)
    terms = pltpu.VMEM((K * R, 2 * D), BF16)
    dma = pltpu.SemaphoreType.DMA
    masked, h0, live = call(
        mask_dead,
        [("v", row), ("w", row), ("w", row)],
        [pltpu.SMEM((1, 1), jnp.int32), dma((2,))],
        [("a", bin_counts), ("h", initial_latents[0, 0])],
    )
    first, second = neighbours_along_gx(masked)
    w, wt, idx, idxt, cot = call(
        prepare,
        [
            ("w", pairs, BF16), ("w", pairs, BF16), ("w", big, jnp.int32), ("w", (K, R), jnp.int32),
            ("w", row),
        ],
        [vmem(2, 6 * D, D), pltpu.VMEM((K, R), jnp.int32), dma((7,))],
        [
            ("s", flags), ("h", raw),
            ("h", w_send), ("h", w_receive), ("h", w_edge), ("h", w_node), ("h", w_update),
            ("h", final_cotangent[0, 0]),
        ],
    )
    first, second, w, idx = lax.optimization_barrier((first, second, w, idx))
    ta, to, tb = neighbours_along_gy(first, masked, second)
    half = pltpu.VMEM((3 * R, 2 * D), BF16)
    part, column_bins = call(
        column_0,
        [("w", big), ("w", table3)],
        [half],
        [("s", flags), ("v", to), ("w", idx), ("w", h0), ("w", w)],
    )
    part, partner_bins = call(
        partner_0,
        [("w", big), ("w", table3)],
        [half],
        [("s", flags), *(("v", a) for a in ta), ("w", idx), ("w", part), ("w", w)],
        1e-6,
    )
    send1, slope0, next_bins, kept = call(
        forward_0,
        [("v", row), ("w", big), ("w", table3), ("w", (6, R, D))],
        [half],
        [("s", flags), ("v", tb), ("w", idx), ("w", part), ("w", h0), ("w", live), ("w", w)],
    )
    slope0, bins0, saved = call(
        forward_0_rest,
        [("h", big), ("h", bins9), ("w", (8, R, D))],
        [dma((4,))],
        [("w", kept), ("w", slope0), ("w", partner_bins), ("w", column_bins), ("w", next_bins), ("w", w)],
    )
    first, second = neighbours_along_gx(send1)
    first, second, saved = lax.optimization_barrier((first, second, saved))
    ta, to, tb = neighbours_along_gy(first, send1, second)
    (part,) = call(
        column_1, [("w", big)], [half], [("s", flags), ("v", to), ("w", idx), ("w", saved)]
    )
    (part,) = call(
        partner_1, [("w", big)], [half], [("s", flags), *(("v", a) for a in ta), ("w", idx), ("w", part)], 1e-6
    )
    pa, pb, terms1, kept = call(
        middle_1,
        [("v", table3), ("v", table3), ("w", (K * R, 2 * D), BF16), ("w", (7, R, D))],
        [half, vmem(*big)],
        [
            ("s", flags), ("v", tb), ("w", idx), ("w", idxt), ("w", part), ("w", saved), ("w", cot),
            ("w", live), ("w", w), ("w", wt),
        ],
    )
    ra, rb = along_gy(pa, pb)
    leave = (CHIPS * CAP, D)
    po, h2, rows_keep, rows_send, g1 = call(
        middle_1_rest,
        [("v", table3), ("h", row), ("w", leave), ("w", leave), ("w", rows6)],
        [vmem(*row), dma],
        [
            ("s", flags), ("w", idxt), ("w", terms1), ("w", kept), ("w", saved), ("w", w), ("w", wt),
            ("v", leave_rows[0, 0].T), ("v", leave_counts[0]),
        ],
    )
    rows_got = swap(rows_send, "gy", False)
    low, mo, high = columns(ra, po, rb)
    mb = swap(high, "gx", True)
    ma = swap(low, "gx", False)
    ma, mb, rows_got = lax.optimization_barrier((ma, mb, rows_got))
    pa, pb, po, sums0, parts0, bins0 = call(
        backward_0,
        [("w", table3), ("w", table3), ("w", table3), ("w", bins9), ("w", (4, R, D)), ("w", bins9)],
        [terms, vmem(*big), dma((2,))],
        [
            ("w", idxt), ("v", ma), ("v", mo), ("v", mb), ("w", saved), ("h", slope0),
            ("h", bins0), ("w", g1), ("w", live), ("w", wt),
        ],
    )
    g_keep, *g_send = call(
        grads_0,
        [("w", rows6)] + [("w", ((b - a) * PIECE, D)) for a, b in zip(CUTS, CUTS[1:])],
        [vmem(2, 6 * D, D)],
        [
            ("s", flags), ("w", saved), ("w", bins0), ("w", sums0), ("w", parts0), ("w", h0), ("w", g1), ("w", wt),
        ],
        5.0,
    )
    g_got = [swap(g, "gy", False) for g in g_send]
    ra, rb = along_gy(pa, pb)
    (outgoing,) = call(
        tail_pack,
        [("v", (CHIPS * EACH, D))],
        [],
        [("s", flags), ("v", rows_keep), ("v", rows_got), ("v", g_keep), *(("v", g) for g in g_got)],
        0.01,
    )
    outgoing, ra, rb = lax.optimization_barrier((outgoing, ra, rb))
    arrived = exchange(outgoing)
    (pieces,) = call(tail_sum, [("v", (CHIPS * PIECE, D))], [], [("v", arrived)])
    own = exchange(pieces)
    low, mid, high = columns(ra, po, rb)
    second = swap(high, "gx", True)
    first = swap(low, "gx", False)
    (arrivals,) = call(
        take_arrivals,
        [("h", (DEVICES * CAP, D))],
        [vmem(DEVICES * CAP, D), dma],
        [("v", arrived)],
    )
    own, first, second, arrivals = lax.optimization_barrier((own, first, second, arrivals))
    grad_initial = first + mid + second
    partner = swap(own, "gy", False)
    sums = call(
        tail_split,
        [("h", two), ("h", two), ("h", two), ("h", (2, 2 * D, D)), ("h", two)],
        [dma((10,))],
        [("s", flags), ("v", own), ("v", partner)],
    )
    return (
        h2.reshape(1, 1, R, D),
        arrivals.reshape(1, 1, DEVICES, CAP, D),
        grad_initial.reshape(1, 1, R, D),
        *sums,
    )


def solution(mesh):
    in_specs = (
        P("gx", "gy", None, None),
        P("gx", "gy", None, None),
        P("gx", "gy"),
        P("gx", "gy", None, None),
        P("gx", "gy", None, None),
        P("gx", "gy", None),
        P(),
        P(),
        P(),
        P(),
        P(),
    )
    out_specs = (
        P("gx", "gy", None, None),
        P("gx", "gy", None, None, None),
        P("gx", "gy", None, None),
        P(),
        P(),
        P(),
        P(),
        P(),
    )
    return jax.shard_map(body, mesh=mesh, in_specs=in_specs, out_specs=out_specs, check_vma=False)
```

```python
import jax
import jax.numpy as jnp
from jax import lax
from jax.experimental import pallas as pl
from jax.experimental.pallas import tpu as pltpu
from jax.sharding import PartitionSpec as P

EPS = 1e-05
AXES = ("gx", "gy")
GX, GY = 16, 8
DEVICES = GX * GY
CHIPS = DEVICES // 2
D = 128
R = 128
K = 24
BLOCKS = 9
CAP = 8
PIECE = 6 * D // CHIPS
EACH = 2 * CAP + PIECE
CUTS = (0, 22, 44, CHIPS)
SEND, RECV, EDGE, NODE, UPDATE, EDGE_NODE = 0, 1, 2, 3, 5, 6
FLAG = 1e30
NEVER = -1e30
VMEM_BYTES = 12 * 1024 * 1024
F32, BF16 = jnp.float32, jnp.bfloat16


def halves(a):
    high = a.astype(BF16)
    return high, (a - high.astype(F32)).astype(BF16)


def fold(wide):
    n = wide.shape[1] // 2
    return wide[:, :n] + wide[:, n:]


def pair(b):
    bh, bl = halves(b)
    both = jnp.concatenate([bh, bl], 1)
    return jnp.concatenate([both, both], 0)


def mm(a, paired):
    return fold(jnp.dot(jnp.concatenate(halves(a), 1), paired, preferred_element_type=F32))


def mm_tn(a, b):
    return fold(
        lax.dot_general(
            jnp.concatenate(halves(a), 0),
            pair(b),
            (((0,), (0,)), ((), ())),
            preferred_element_type=F32,
        )
    )


def sigmoid(v):
    return 0.5 + 0.5 * jnp.tanh(0.5 * v)


def silu_and_slope(v):
    s = sigmoid(v)
    t = v * s
    return t, s + t * (1.0 - s)


def block_limits(flags):
    return [
        [
            jnp.where(((xs < 2) | (flags[0] > 0)) & ((ys < 2) | (flags[1] > 0)), 1e20, -1e20)
            for xs in range(3)
        ]
        for ys in range(3)
    ]


def hot_rows(idx, k, blocks):
    lanes = lax.broadcasted_iota(jnp.int32, (R, R), 1)
    return jnp.concatenate(
        [jnp.where(idx[k] == lanes + b * R, 1.0, 0.0).astype(BF16) for b in blocks], 1
    )


def hot_columns(idxt, k, first, count):
    line = lax.broadcast_in_dim(idxt[k : k + 1, :], (count, R), (0, 1))
    rows = lax.broadcasted_iota(jnp.int32, (count, R), 0) + first
    return jnp.where(line == rows, 1.0, 0.0).astype(BF16)


PARTNER, COLUMN, NEXT = (0, 1, 2), (3, 4, 5), (6, 7, 8)


def edge_gather(idx, table, blocks, start, wide):
    hot = jnp.concatenate([hot_rows(idx, start + j, blocks) for j in range(wide)], 0)
    return fold(jnp.dot(hot, table[...], preferred_element_type=F32))


def edge_add(idx, table, blocks, more, part):
    for start in range(0, K, 8):
        got = edge_gather(idx, table, blocks, start, 8)
        for j in range(8):
            part[start + j] = got[j * R : (j + 1) * R] + more(start + j)


def edge_forward(idx, table, part, slope_ref, start, wide, total):
    got = edge_gather(idx, table, NEXT, start, wide)
    for j in range(wide):
        t, slope = silu_and_slope(got[j * R : (j + 1) * R] + part[start + j])
        total = total + t
        slope_ref[start + j] = slope
    return total


def edge_terms(slope_ref, back, terms_ref):
    total = jnp.zeros((R, D), F32)
    for k in range(K):
        d = back * slope_ref[k]
        total = total + d
        high, low = halves(d)
        terms_ref[k * R : (k + 1) * R, 0:D] = high
        terms_ref[k * R : (k + 1) * R, D : 2 * D] = low
    return total


def edge_scatter(idxt, terms_ref, first, count):
    hot = jnp.concatenate([hot_columns(idxt, k, first * R, count * R) for k in range(K)], 1)
    return fold(jnp.dot(hot, terms_ref[...], preferred_element_type=F32))


def node_forward(h, hidden, live, w, step):
    a = mm(h, w[step, NODE]) + mm(hidden, w[step, EDGE_NODE])
    inner, slope = silu_and_slope(a)
    u = mm(inner, w[step, UPDATE])
    c = u - jnp.mean(u, axis=1, keepdims=True)
    scale = lax.rsqrt(jnp.mean(c * c, axis=1, keepdims=True) + EPS)
    n = c * scale
    return h + live * n, inner, slope, n, scale


def node_backward(dh, live, slope, n, scale, wt, step):
    dn = live * dh
    du = scale * (
        dn - jnp.mean(dn, axis=1, keepdims=True) - n * jnp.mean(dn * n, axis=1, keepdims=True)
    )
    da = mm(du, wt[step, UPDATE]) * slope
    back = mm(da, wt[step, EDGE_NODE])
    return du, da, back, dh + mm(da, wt[step, NODE])


def weight_grads(h, hidden, message, inner, du, da, dmessage, drecv):
    return (
        mm_tn(h, drecv),
        mm_tn(hidden, dmessage),
        mm_tn(h, da),
        mm_tn(message, da),
        mm_tn(inner, du),
    )


def mask_dead(counts, h_in, masked, h, live, count, sems):
    copies = [
        pltpu.make_async_copy(counts, count, sems.at[0]),
        pltpu.make_async_copy(h_in, h, sems.at[1]),
    ]
    for copy in copies:
        copy.start()
    for copy in copies:
        copy.wait()
    rows = lax.broadcasted_iota(jnp.int32, (R, D), 0)
    masked[...] = jnp.where(rows < count[0, 0], h[...], FLAG)
    live[...] = jnp.where(rows < count[0, 0], 1.0, 0.0)


def prepare(
    flags, raw_in, send, recv, edge, node, update, cot,
    w, wt, idx, idxt, cot_out,
    f, raw, sems,
):
    copies = [
        pltpu.make_async_copy(src, dst, sems.at[i])
        for i, (src, dst) in enumerate(
            (
                (send, f.at[:, 0:D]),
                (recv, f.at[:, D : 2 * D]),
                (edge, f.at[:, 2 * D : 3 * D]),
                (node, f.at[:, 3 * D : 5 * D]),
                (update, f.at[:, 5 * D : 6 * D]),
                (cot, cot_out),
                (raw_in, raw),
            )
        )
    ]
    for copy in copies:
        copy.start()
    copies.pop().wait()
    place = raw[...] // R
    px = (place >= 3).astype(jnp.int32) + (place >= 6).astype(jnp.int32)
    py = place - 3 * px
    xs = jnp.where(flags[3] == 0, 2 - px, px)
    ys = jnp.where(flags[2] == 0, 2 - py, py)
    slot = (ys * 3 + xs) * R + raw[...] - place * R
    idxt[...] = slot
    tall = jnp.concatenate([slot.astype(F32), jnp.zeros((R - K, R), F32)], 0)
    tall = tall.T.astype(jnp.int32)
    for k in range(K):
        idx[k] = lax.broadcast_in_dim(tall[:, k : k + 1], (R, R), (0, 1))
    for copy in copies:
        copy.wait()
    for step in range(2):
        for m in range(6):
            v = f[step, m * D : (m + 1) * D]
            w[step, m] = pair(v)
            wt[step, m] = pair(v.T)
        both = mm(f[step, 2 * D : 3 * D], w[step, NODE + 1])
        w[step, EDGE_NODE] = pair(both)
        wt[step, EDGE_NODE] = pair(both.T)


def fill(table, at, sent):
    high, low = halves(sent)
    table[at * R : (at + 1) * R, 0:D] = high
    table[at * R : (at + 1) * R, D : 2 * D] = low


def project(refs, limits, w, bins, table):
    for xs in range(3):
        v = refs[xs][...]
        keep = v < limits[xs]
        b = jnp.where(keep, v, 0.0)
        bins[xs] = b
        fill(table, xs, jnp.where(keep, mm(b, w[0, SEND]), NEVER))


def column_0(flags, to, idx, h, w, part, bins, table):
    project([to.at[xs] for xs in range(3)], block_limits(flags)[1], w, bins, table)
    receiver = mm(h[...], w[0, RECV])
    edge_add(idx, table, COLUMN, lambda k: receiver, part)


def partner_0(flags, t0, t1, t2, idx, part_in, w, part, bins, table):
    project((t0, t1, t2), block_limits(flags)[0], w, bins, table)
    edge_add(idx, table, PARTNER, lambda k: part_in[k], part)


def forward_0(
    flags, tb, idx, part, h, live_in, w,
    send_out, slope, bins, kept,
    table,
):
    project([tb.at[xs] for xs in range(3)], block_limits(flags)[2], w, bins, table)
    h0, live = h[...], live_in[...]
    hidden = jnp.zeros((R, D), F32)
    for start in range(0, K, 8):
        hidden = edge_forward(idx, table, part, slope, start, 8, hidden)
    h1, inner, islope, n, scale = node_forward(h0, hidden, live, w, 0)
    send_out[...] = jnp.where(live > 0, mm(h1, w[1, SEND]), NEVER)
    for i, value in enumerate((h1, hidden, inner, islope, n)):
        kept[i] = value
    kept[5] = lax.broadcast_in_dim(scale, (R, D), (0, 1))


def forward_0_rest(kept, slope, partner, column, across, w, slope_out, bins_out, saved, sems):
    copies = [
        pltpu.make_async_copy(slope, slope_out, sems.at[0]),
        pltpu.make_async_copy(partner, bins_out.at[0:3], sems.at[1]),
        pltpu.make_async_copy(column, bins_out.at[3:6], sems.at[2]),
        pltpu.make_async_copy(across, bins_out.at[6:9], sems.at[3]),
    ]
    for copy in copies:
        copy.start()
    saved[0] = kept[0]
    saved[1] = mm(kept[0], w[1, RECV])
    saved[2] = kept[1]
    saved[3] = mm(kept[1], w[0, EDGE])
    for i in range(2, 6):
        saved[i + 2] = kept[i]
    for copy in copies:
        copy.wait()


def mask_sent(refs, limits, table):
    for xs in range(3):
        fill(table, xs, jnp.where(limits[xs] > 0, refs[xs][...], NEVER))


def column_1(flags, to, idx, saved, part, table):
    mask_sent([to.at[xs] for xs in range(3)], block_limits(flags)[1], table)
    edge_add(idx, table, COLUMN, lambda k: saved[1], part)


def partner_1(flags, t0, t1, t2, idx, part_in, part, table):
    mask_sent((t0, t1, t2), block_limits(flags)[0], table)
    edge_add(idx, table, PARTNER, lambda k: part_in[k], part)


def middle_1(
    flags, tb, idx, idxt, part, saved, cot, live_in, w, wt,
    pa0, pa1, pa2, pb, terms, kept,
    table, slope,
):
    mask_sent([tb.at[xs] for xs in range(3)], block_limits(flags)[2], table)
    hidden = jnp.zeros((R, D), F32)
    for start in range(0, K, 8):
        hidden = edge_forward(idx, table, part, slope, start, 8, hidden)
    h1, live = saved[0], live_in[...]
    new, inner, islope, n, scale = node_forward(h1, hidden, live, w, 1)
    du, da, back, dh1 = node_backward(cot[...], live, islope, n, scale, wt, 1)
    drecv = edge_terms(slope, back, terms)
    got = edge_scatter(idxt, terms, 0, 3)
    for xs, out in enumerate((pa0, pa1, pa2)):
        out[...] = got[xs * R : (xs + 1) * R]
    pb[...] = edge_scatter(idxt, terms, 6, 3).reshape(3, R, D)
    for i, value in enumerate((hidden, inner, du, da, drecv, dh1, new)):
        kept[i] = value


def middle_1_rest(
    flags, idxt, terms, kept, saved, w, wt, leave_rows, leave_counts,
    po, h_out, rows_keep, rows_send, g,
    h2, sem,
):
    hidden, inner, du, da, drecv, dh1, new = (kept[i] for i in range(7))
    h2[...] = new
    copy = pltpu.make_async_copy(h2, h_out, sem)
    copy.start()
    pack_leaving(flags, leave_rows, leave_counts, new, rows_keep, rows_send)
    po[...] = edge_scatter(idxt, terms, 3, 3).reshape(3, R, D)
    message = mm(hidden, w[1, EDGE])
    dmessage = mm(da, wt[1, NODE + 1])
    grads = weight_grads(saved[0], hidden, message, inner, du, da, dmessage, drecv)
    for i, value in enumerate(grads):
        g[i * D : (i + 1) * D] = value
    g[5 * D :] = dh1 + mm(drecv, wt[1, RECV])
    copy.wait()


def backward_0(
    idxt, ma, mo, mb, saved, slope_in, bins_in, g1, live, wt,
    pa, pb, po, sums, terms_out, bins,
    terms, slope, sems,
):
    copies = [
        pltpu.make_async_copy(src, dst, sems.at[i])
        for i, (src, dst) in enumerate(
            (
                (slope_in, slope),
                (bins_in, bins),
            )
        )
    ]
    for copy in copies:
        copy.start()
    dsend = ma[...] + mo[...] + mb[...]
    dh1 = g1[5 * D :] + mm(dsend, wt[1, SEND])
    du, da, back, dh0 = node_backward(dh1, live[...], saved[5], saved[6], saved[7][:, 0:1], wt, 0)
    copies[0].wait()
    drecv = edge_terms(slope, back, terms)
    got = edge_scatter(idxt, terms, 0, BLOCKS)
    for part, out in enumerate((pa, po, pb)):
        for xs in range(3):
            v = got[(part * 3 + xs) * R : (part * 3 + xs + 1) * R]
            sums[part * 3 + xs] = v
            out[xs] = mm(v, wt[0, SEND])
    po[1] += dh0 + mm(drecv, wt[0, RECV])
    terms_out[0] = du
    terms_out[1] = da
    terms_out[2] = drecv
    terms_out[3] = dsend
    for copy in copies[1:]:
        copy.wait()


def grads_0(flags, saved, bins, sums, parts, h, g1, wt, keep, *rest):
    *send, g = rest
    du, da, drecv, dsend = (parts[i] for i in range(4))
    dmessage = mm(da, wt[0, NODE + 1])
    total = mm_tn(bins[0], sums[0])
    for b in range(1, BLOCKS):
        total = total + mm_tn(bins[b], sums[b])
    g[0, 0:D] = total
    grads = weight_grads(h[...], saved[2], saved[3], saved[4], du, da, dmessage, drecv)
    for i, value in enumerate(grads):
        g[0, (i + 1) * D : (i + 2) * D] = value
    g[1, 0:D] = mm_tn(saved[0], dsend)
    g[1, D:] = g1[0 : 5 * D]
    mine = flags[2]
    keep[...] = g[mine]
    for out, first, last in zip(send, CUTS, CUTS[1:]):
        out[...] = g[1 - mine, first * PIECE : last * PIECE]


def pack_leaving(flags, rows, counts, h, keep, send):
    q = lax.broadcasted_iota(jnp.int32, (CAP, DEVICES), 0)
    rows = jnp.where(q < lax.broadcast_in_dim(counts[...], (CAP, DEVICES), (0, 1)), rows[...], -1)
    target = lax.broadcasted_iota(jnp.int32, (DEVICES, DEVICES), 0)
    at = lax.broadcasted_iota(jnp.int32, (DEVICES, DEVICES), 1)
    first = at < CHIPS
    wanted = jnp.where(first, 2 * at + flags[2], 2 * (at - CHIPS) + 1 - flags[2])
    order = jnp.where(target == wanted, 1.0, 0.0).astype(BF16)
    rows = jnp.dot(rows.astype(F32).astype(BF16), order, preferred_element_type=F32)
    rows = rows.astype(jnp.int32)
    paired = jnp.concatenate(halves(h), 1)
    slots = lax.broadcasted_iota(jnp.int32, (R, DEVICES), 0)
    for c in range(CAP):
        line = lax.broadcast_in_dim(rows[c : c + 1], (R, DEVICES), (0, 1))
        hot = jnp.where(slots == line, 1.0, 0.0).astype(BF16)
        got = fold(
            lax.dot_general(hot, paired, (((0,), (0,)), ((), ())), preferred_element_type=F32)
        )
        keep[c * CHIPS : (c + 1) * CHIPS] = got[:CHIPS]
        send[c * CHIPS : (c + 1) * CHIPS] = got[CHIPS:]


def tail_pack(flags, rows_keep, rows_got, g_keep, *rest):
    *g_got, out = rest
    even = flags[2] == 0
    for q in range(CAP):
        at = slice(q * CHIPS, (q + 1) * CHIPS)
        out[pl.ds(q, CHIPS, stride=EACH)] = jnp.where(even, rows_keep[at], rows_got[at])
        out[pl.ds(CAP + q, CHIPS, stride=EACH)] = jnp.where(even, rows_got[at], rows_keep[at])
    for got, first, last in zip(g_got, CUTS, CUTS[1:]):
        for i in range(first, last):
            near = got[(i - first) * PIECE : (i - first + 1) * PIECE]
            out[i * EACH + 2 * CAP : (i + 1) * EACH] = g_keep[i * PIECE : (i + 1) * PIECE] + near


def tail_sum(arrived, out):
    for q in range(PIECE):
        rows = arrived[pl.ds(2 * CAP + q, CHIPS, stride=EACH)]
        total = jnp.sum(rows, axis=0, keepdims=True)
        out[pl.ds(q, CHIPS, stride=PIECE)] = lax.broadcast_in_dim(total, (CHIPS, D), (0, 1))


def take_arrivals(arrived, out, rows, sem):
    for i in range(CHIPS):
        rows[i * 2 * CAP : (i + 1) * 2 * CAP] = arrived[i * EACH : i * EACH + 2 * CAP]
    copy = pltpu.make_async_copy(rows, out, sem)
    copy.start()
    copy.wait()


def tail_split(flags, own, other, o_send, o_recv, o_edge, o_node, o_update, sems):
    mine = flags[2]
    copies = []
    for out, at, size in (
        (o_send, 0, D),
        (o_recv, D, D),
        (o_edge, 2 * D, D),
        (o_node, 3 * D, 2 * D),
        (o_update, 5 * D, D),
    ):
        for rows, step in ((own, mine), (other, 1 - mine)):
            copies.append(
                pltpu.make_async_copy(rows.at[at : at + size], out.at[step], sems.at[len(copies)])
            )
            copies[-1].start()
    for copy in copies:
        copy.wait()


def vmem(*shape):
    return pltpu.VMEM(shape, F32)


def call(kernel, outs, scratch, args, microseconds=1.0):
    places = {"s": pltpu.SMEM, "v": pltpu.VMEM, "w": pltpu.VMEM, "h": pltpu.HBM, "a": pl.ANY}
    return pl.pallas_call(
        kernel,
        out_shape=[
            {"h": pltpu.HBM, "w": pltpu.VMEM, "v": jax.ShapeDtypeStruct}[p](shape, *(kind or (F32,)))
            for p, shape, *kind in outs
        ],
        in_specs=[pl.BlockSpec(memory_space=places[p]) for p, _ in args],
        out_specs=[pl.BlockSpec(memory_space=places[p]) for p, *_ in outs],
        scratch_shapes=scratch,
        compiler_params=pltpu.CompilerParams(vmem_limit_bytes=VMEM_BYTES),
        cost_estimate=pl.CostEstimate(
            flops=int(microseconds * 1e9), bytes_accessed=int(microseconds * 3e6), transcendentals=0
        ),
    )(
        *[
            pltpu.with_memory_space_constraint(a, places[p]) if p in "hw" else a
            for p, a in args
        ]
    )


def swap(a, axis, second):
    n = lax.axis_size(axis)
    if not second:
        return lax.ppermute(a, axis, [(i, i ^ 1) for i in range(n)])
    pairs = [(i, (i + 1) % n if i % 2 else (i - 1) % n) for i in range(n)]
    if axis == "gy":
        return lax.ppermute(a, axis, pairs)
    return lax.ppermute(
        a,
        AXES,
        [
            (x * GY + y, x * GY + (y ^ 1) if x in (0, n - 1) else to * GY + y)
            for x, to in pairs
            for y in range(GY)
        ],
    )


def neighbours_along_gx(own):
    return swap(own, "gx", False), swap(own, "gx", True)


def neighbours_along_gy(first, own, second):
    column = jnp.stack([first, own, second])
    return [swap(a, "gy", False) for a in (first, own, second)], column, swap(column, "gy", True)


def along_gy(pa, pb):
    return swap(pa, "gy", False), swap(pb, "gy", True)


def columns(ra, po, rb):
    return po[0] + ra[0] + rb[0], po[1] + ra[1] + rb[1], po[2] + ra[2] + rb[2]


def exchange(a):
    groups = [[2 * chip + core for chip in range(CHIPS)] for core in range(2)]
    moved = lax.all_to_all(
        a.reshape(CHIPS, 1, -1),
        AXES,
        split_axis=0,
        concat_axis=0,
        tiled=True,
        axis_index_groups=groups,
    )
    return moved.reshape(a.shape)


def body(
    initial_latents,
    final_cotangent,
    bin_counts,
    neighbours,
    leave_rows,
    leave_counts,
    w_send,
    w_receive,
    w_edge,
    w_node,
    w_update,
):
    gx, gy = lax.axis_index("gx"), lax.axis_index("gy")
    core = gy % 2
    flags = jnp.stack(
        [
            ((gx > 0) & (gx < GX - 1)).astype(jnp.int32),
            ((gy > 0) & (gy < GY - 1)).astype(jnp.int32),
            core,
            gx % 2,
        ]
    )
    raw = neighbours[0, 0].T
    row, table3, big, bins9 = (R, D), (3, R, D), (K, R, D), (BLOCKS, R, D)
    two, rows6, pairs = (2, R, D), (6 * D, D), (2, 7, 2 * D, 2 * D)
    terms = pltpu.VMEM((K * R, 2 * D), BF16)
    dma = pltpu.SemaphoreType.DMA
    masked, h0, live = call(
        mask_dead,
        [("v", row), ("w", row), ("w", row)],
        [pltpu.SMEM((1, 1), jnp.int32), dma((2,))],
        [("a", bin_counts), ("h", initial_latents[0, 0])],
    )
    first, second = neighbours_along_gx(masked)
    w, wt, idx, idxt, cot = call(
        prepare,
        [
            ("w", pairs, BF16), ("w", pairs, BF16), ("w", big, jnp.int32), ("w", (K, R), jnp.int32),
            ("w", row),
        ],
        [vmem(2, 6 * D, D), pltpu.VMEM((K, R), jnp.int32), dma((7,))],
        [
            ("s", flags), ("h", raw),
            ("h", w_send), ("h", w_receive), ("h", w_edge), ("h", w_node), ("h", w_update),
            ("h", final_cotangent[0, 0]),
        ],
    )
    first, second, w, idx = lax.optimization_barrier((first, second, w, idx))
    ta, to, tb = neighbours_along_gy(first, masked, second)
    half = pltpu.VMEM((3 * R, 2 * D), BF16)
    part, column_bins = call(
        column_0,
        [("w", big), ("w", table3)],
        [half],
        [("s", flags), ("v", to), ("w", idx), ("w", h0), ("w", w)],
    )
    part, partner_bins = call(
        partner_0,
        [("w", big), ("w", table3)],
        [half],
        [("s", flags), *(("v", a) for a in ta), ("w", idx), ("w", part), ("w", w)],
        1e-6,
    )
    send1, slope0, next_bins, kept = call(
        forward_0,
        [("v", row), ("w", big), ("w", table3), ("w", (6, R, D))],
        [half],
        [("s", flags), ("v", tb), ("w", idx), ("w", part), ("w", h0), ("w", live), ("w", w)],
    )
    slope0, bins0, saved = call(
        forward_0_rest,
        [("h", big), ("h", bins9), ("w", (8, R, D))],
        [dma((4,))],
        [("w", kept), ("w", slope0), ("w", partner_bins), ("w", column_bins), ("w", next_bins), ("w", w)],
    )
    first, second = neighbours_along_gx(send1)
    first, second, saved = lax.optimization_barrier((first, second, saved))
    ta, to, tb = neighbours_along_gy(first, send1, second)
    (part,) = call(
        column_1, [("w", big)], [half], [("s", flags), ("v", to), ("w", idx), ("w", saved)]
    )
    (part,) = call(
        partner_1, [("w", big)], [half], [("s", flags), *(("v", a) for a in ta), ("w", idx), ("w", part)], 1e-6
    )
    *pa, pb, terms1, kept = call(
        middle_1,
        [("v", row)] * 3 + [("v", table3), ("w", (K * R, 2 * D), BF16), ("w", (7, R, D))],
        [half, vmem(*big)],
        [
            ("s", flags), ("v", tb), ("w", idx), ("w", idxt), ("w", part), ("w", saved), ("w", cot),
            ("w", live), ("w", w), ("w", wt),
        ],
    )
    rb = swap(pb, "gy", True)
    ra = [swap(a, "gy", False) for a in pa]
    leave = (CHIPS * CAP, D)
    po, h2, rows_keep, rows_send, g1 = call(
        middle_1_rest,
        [("v", table3), ("h", row), ("w", leave), ("w", leave), ("w", rows6)],
        [vmem(*row), dma],
        [
            ("s", flags), ("w", idxt), ("w", terms1), ("w", kept), ("w", saved), ("w", w), ("w", wt),
            ("v", leave_rows[0, 0].T), ("v", leave_counts[0]),
        ],
    )
    rows_got = swap(rows_send, "gy", False)
    low, mo, high = columns(ra, po, rb)
    mb = swap(high, "gx", True)
    ma = swap(low, "gx", False)
    ma, mb, rows_got = lax.optimization_barrier((ma, mb, rows_got))
    pa, pb, po, sums0, parts0, bins0 = call(
        backward_0,
        [("w", table3), ("w", table3), ("w", table3), ("w", bins9), ("w", (4, R, D)), ("w", bins9)],
        [terms, vmem(*big), dma((2,))],
        [
            ("w", idxt), ("v", ma), ("v", mo), ("v", mb), ("w", saved), ("h", slope0),
            ("h", bins0), ("w", g1), ("w", live), ("w", wt),
        ],
    )
    g_keep, *g_send = call(
        grads_0,
        [("w", rows6)] + [("w", ((b - a) * PIECE, D)) for a, b in zip(CUTS, CUTS[1:])],
        [vmem(2, 6 * D, D)],
        [
            ("s", flags), ("w", saved), ("w", bins0), ("w", sums0), ("w", parts0), ("w", h0), ("w", g1), ("w", wt),
        ],
        5.0,
    )
    g_got = [swap(g, "gy", False) for g in g_send]
    ra, rb = along_gy(pa, pb)
    (outgoing,) = call(
        tail_pack,
        [("v", (CHIPS * EACH, D))],
        [],
        [("s", flags), ("v", rows_keep), ("v", rows_got), ("v", g_keep), *(("v", g) for g in g_got)],
        0.01,
    )
    outgoing, ra, rb = lax.optimization_barrier((outgoing, ra, rb))
    arrived = exchange(outgoing)
    (pieces,) = call(tail_sum, [("v", (CHIPS * PIECE, D))], [], [("v", arrived)])
    own = exchange(pieces)
    low, mid, high = columns(ra, po, rb)
    second = swap(high, "gx", True)
    first = swap(low, "gx", False)
    (arrivals,) = call(
        take_arrivals,
        [("h", (DEVICES * CAP, D))],
        [vmem(DEVICES * CAP, D), dma],
        [("v", arrived)],
    )
    own, first, second, arrivals = lax.optimization_barrier((own, first, second, arrivals))
    grad_initial = first + mid + second
    partner = swap(own, "gy", False)
    sums = call(
        tail_split,
        [("h", two), ("h", two), ("h", two), ("h", (2, 2 * D, D)), ("h", two)],
        [dma((10,))],
        [("s", flags), ("v", own), ("v", partner)],
    )
    return (
        h2.reshape(1, 1, R, D),
        arrivals.reshape(1, 1, DEVICES, CAP, D),
        grad_initial.reshape(1, 1, R, D),
        *sums,
    )


def solution(mesh):
    in_specs = (
        P("gx", "gy", None, None),
        P("gx", "gy", None, None),
        P("gx", "gy"),
        P("gx", "gy", None, None),
        P("gx", "gy", None, None),
        P("gx", "gy", None),
        P(),
        P(),
        P(),
        P(),
        P(),
    )
    out_specs = (
        P("gx", "gy", None, None),
        P("gx", "gy", None, None, None),
        P("gx", "gy", None, None),
        P(),
        P(),
        P(),
        P(),
        P(),
    )
    return jax.shard_map(body, mesh=mesh, in_specs=in_specs, out_specs=out_specs, check_vma=False)
```

```python
import jax
import jax.numpy as jnp
from jax import lax
from jax.experimental import pallas as pl
from jax.experimental.pallas import tpu as pltpu
from jax.sharding import PartitionSpec as P

EPS = 1e-05
AXES = ("gx", "gy")
GX, GY = 16, 8
DEVICES = GX * GY
CHIPS = DEVICES // 2
D = 128
R = 128
K = 24
BLOCKS = 9
CAP = 8
PIECE = 6 * D // CHIPS
EACH = 2 * CAP + PIECE
CUTS = (0, 22, 44, CHIPS)
SEND, RECV, EDGE, NODE, UPDATE, EDGE_NODE = 0, 1, 2, 3, 5, 6
FLAG = 1e30
NEVER = -1e30
VMEM_BYTES = 12 * 1024 * 1024
F32, BF16 = jnp.float32, jnp.bfloat16


def halves(a):
    high = a.astype(BF16)
    return high, (a - high.astype(F32)).astype(BF16)


def fold(wide):
    n = wide.shape[1] // 2
    return wide[:, :n] + wide[:, n:]


def pair(b):
    bh, bl = halves(b)
    both = jnp.concatenate([bh, bl], 1)
    return jnp.concatenate([both, both], 0)


def mm(a, paired):
    return fold(jnp.dot(jnp.concatenate(halves(a), 1), paired, preferred_element_type=F32))


def mm_tn(a, b):
    return fold(
        lax.dot_general(
            jnp.concatenate(halves(a), 0),
            pair(b),
            (((0,), (0,)), ((), ())),
            preferred_element_type=F32,
        )
    )


def sigmoid(v):
    return 0.5 + 0.5 * jnp.tanh(0.5 * v)


def silu_and_slope(v):
    s = sigmoid(v)
    t = v * s
    return t, s + t * (1.0 - s)


def block_limits(flags):
    return [
        [
            jnp.where(((xs < 2) | (flags[0] > 0)) & ((ys < 2) | (flags[1] > 0)), 1e20, -1e20)
            for xs in range(3)
        ]
        for ys in range(3)
    ]


def hot_rows(idx, k, blocks):
    lanes = lax.broadcasted_iota(jnp.int32, (R, R), 1)
    return jnp.concatenate(
        [jnp.where(idx[k] == lanes + b * R, 1.0, 0.0).astype(BF16) for b in blocks], 1
    )


def hot_columns(idxt, k, first, count):
    line = lax.broadcast_in_dim(idxt[k : k + 1, :], (count, R), (0, 1))
    rows = lax.broadcasted_iota(jnp.int32, (count, R), 0) + first
    return jnp.where(line == rows, 1.0, 0.0).astype(BF16)


PARTNER, COLUMN, NEXT = (0, 1, 2), (3, 4, 5), (6, 7, 8)


def edge_gather(idx, table, blocks, start, wide):
    hot = jnp.concatenate([hot_rows(idx, start + j, blocks) for j in range(wide)], 0)
    return fold(jnp.dot(hot, table[...], preferred_element_type=F32))


def edge_add(idx, table, blocks, more, part):
    for start in range(0, K, 8):
        got = edge_gather(idx, table, blocks, start, 8)
        for j in range(8):
            part[start + j] = got[j * R : (j + 1) * R] + more(start + j)


def edge_forward(idx, table, part, slope_ref, start, wide, total):
    got = edge_gather(idx, table, NEXT, start, wide)
    for j in range(wide):
        t, slope = silu_and_slope(got[j * R : (j + 1) * R] + part[start + j])
        total = total + t
        slope_ref[start + j] = slope
    return total


def edge_terms(slope_ref, back, terms_ref):
    total = jnp.zeros((R, D), F32)
    for k in range(K):
        d = back * slope_ref[k]
        total = total + d
        high, low = halves(d)
        terms_ref[k * R : (k + 1) * R, 0:D] = high
        terms_ref[k * R : (k + 1) * R, D : 2 * D] = low
    return total


def edge_scatter(idxt, terms_ref, first, count):
    hot = jnp.concatenate([hot_columns(idxt, k, first * R, count * R) for k in range(K)], 1)
    return fold(jnp.dot(hot, terms_ref[...], preferred_element_type=F32))


def node_forward(h, hidden, live, w, step):
    a = mm(h, w[step, NODE]) + mm(hidden, w[step, EDGE_NODE])
    inner, slope = silu_and_slope(a)
    u = mm(inner, w[step, UPDATE])
    c = u - jnp.mean(u, axis=1, keepdims=True)
    scale = lax.rsqrt(jnp.mean(c * c, axis=1, keepdims=True) + EPS)
    n = c * scale
    return h + live * n, inner, slope, n, scale


def node_backward(dh, live, slope, n, scale, wt, step):
    dn = live * dh
    du = scale * (
        dn - jnp.mean(dn, axis=1, keepdims=True) - n * jnp.mean(dn * n, axis=1, keepdims=True)
    )
    da = mm(du, wt[step, UPDATE]) * slope
    back = mm(da, wt[step, EDGE_NODE])
    return du, da, back, dh + mm(da, wt[step, NODE])


def weight_grads(h, hidden, message, inner, du, da, dmessage, drecv):
    return (
        mm_tn(h, drecv),
        mm_tn(hidden, dmessage),
        mm_tn(h, da),
        mm_tn(message, da),
        mm_tn(inner, du),
    )


def mask_dead(counts, h_in, masked, h, live, count, sems):
    copies = [
        pltpu.make_async_copy(counts, count, sems.at[0]),
        pltpu.make_async_copy(h_in, h, sems.at[1]),
    ]
    for copy in copies:
        copy.start()
    for copy in copies:
        copy.wait()
    rows = lax.broadcasted_iota(jnp.int32, (R, D), 0)
    masked[...] = jnp.where(rows < count[0, 0], h[...], FLAG)
    live[...] = jnp.where(rows < count[0, 0], 1.0, 0.0)


def prepare(
    flags, raw_in, send, recv, edge, node, update, cot,
    w, f, idx, idxt, cot_out,
    raw, sems,
):
    copies = [
        pltpu.make_async_copy(src, dst, sems.at[i])
        for i, (src, dst) in enumerate(
            (
                (send, f.at[:, 0:D]),
                (recv, f.at[:, D : 2 * D]),
                (edge, f.at[:, 2 * D : 3 * D]),
                (node, f.at[:, 3 * D : 5 * D]),
                (update, f.at[:, 5 * D : 6 * D]),
                (cot, cot_out),
                (raw_in, raw),
            )
        )
    ]
    for copy in copies:
        copy.start()
    copies.pop().wait()
    place = raw[...] // R
    px = (place >= 3).astype(jnp.int32) + (place >= 6).astype(jnp.int32)
    py = place - 3 * px
    xs = jnp.where(flags[3] == 0, 2 - px, px)
    ys = jnp.where(flags[2] == 0, 2 - py, py)
    slot = (ys * 3 + xs) * R + raw[...] - place * R
    idxt[...] = slot
    tall = jnp.concatenate([slot.astype(F32), jnp.zeros((R - K, R), F32)], 0)
    tall = tall.T.astype(jnp.int32)
    for k in range(K):
        idx[k] = lax.broadcast_in_dim(tall[:, k : k + 1], (R, R), (0, 1))
    for copy in copies:
        copy.wait()
    for step in range(2):
        for m in range(6):
            w[step, m] = pair(f[step, m * D : (m + 1) * D])
        w[step, EDGE_NODE] = pair(mm(f[step, 2 * D : 3 * D], w[step, NODE + 1]))


def prepare_back(f, w, wt):
    for step in range(2):
        for m in range(6):
            wt[step, m] = pair(f[step, m * D : (m + 1) * D].T)
        wt[step, EDGE_NODE] = pair(mm(f[step, 2 * D : 3 * D], w[step, NODE + 1]).T)


def fill(table, at, sent):
    high, low = halves(sent)
    table[at * R : (at + 1) * R, 0:D] = high
    table[at * R : (at + 1) * R, D : 2 * D] = low


def project(refs, limits, w, bins, table):
    for xs in range(3):
        v = refs[xs][...]
        keep = v < limits[xs]
        b = jnp.where(keep, v, 0.0)
        bins[xs] = b
        fill(table, xs, jnp.where(keep, mm(b, w[0, SEND]), NEVER))


def column_0(flags, to, idx, h, w, part, bins, table):
    project([to.at[xs] for xs in range(3)], block_limits(flags)[1], w, bins, table)
    receiver = mm(h[...], w[0, RECV])
    edge_add(idx, table, COLUMN, lambda k: receiver, part)


def partner_0(flags, t0, t1, t2, idx, part_in, w, part, bins, table):
    project((t0, t1, t2), block_limits(flags)[0], w, bins, table)
    edge_add(idx, table, PARTNER, lambda k: part_in[k], part)


def forward_0(
    flags, tb, idx, part, h, live_in, w,
    send_out, slope, bins, kept,
    table,
):
    project([tb.at[xs] for xs in range(3)], block_limits(flags)[2], w, bins, table)
    h0, live = h[...], live_in[...]
    hidden = jnp.zeros((R, D), F32)
    for start in range(0, K, 8):
        hidden = edge_forward(idx, table, part, slope, start, 8, hidden)
    h1, inner, islope, n, scale = node_forward(h0, hidden, live, w, 0)
    send_out[...] = jnp.where(live > 0, mm(h1, w[1, SEND]), NEVER)
    for i, value in enumerate((h1, hidden, inner, islope, n)):
        kept[i] = value
    kept[5] = lax.broadcast_in_dim(scale, (R, D), (0, 1))


def forward_0_rest(kept, slope, partner, column, across, w, slope_out, bins_out, saved, sems):
    copies = [
        pltpu.make_async_copy(slope, slope_out, sems.at[0]),
        pltpu.make_async_copy(partner, bins_out.at[0:3], sems.at[1]),
        pltpu.make_async_copy(column, bins_out.at[3:6], sems.at[2]),
        pltpu.make_async_copy(across, bins_out.at[6:9], sems.at[3]),
    ]
    for copy in copies:
        copy.start()
    saved[0] = kept[0]
    saved[1] = mm(kept[0], w[1, RECV])
    saved[2] = kept[1]
    saved[3] = mm(kept[1], w[0, EDGE])
    for i in range(2, 6):
        saved[i + 2] = kept[i]
    for copy in copies:
        copy.wait()


def mask_sent(refs, limits, table):
    for xs in range(3):
        fill(table, xs, jnp.where(limits[xs] > 0, refs[xs][...], NEVER))


def column_1(flags, to, idx, saved, part, table):
    mask_sent([to.at[xs] for xs in range(3)], block_limits(flags)[1], table)
    edge_add(idx, table, COLUMN, lambda k: saved[1], part)


def partner_1(flags, t0, t1, t2, idx, part_in, part, table):
    mask_sent((t0, t1, t2), block_limits(flags)[0], table)
    edge_add(idx, table, PARTNER, lambda k: part_in[k], part)


def middle_1(
    flags, tb, idx, idxt, part, saved, cot, live_in, w, wt,
    pa0, pa1, pa2, pb, terms, kept,
    table, slope,
):
    mask_sent([tb.at[xs] for xs in range(3)], block_limits(flags)[2], table)
    hidden = jnp.zeros((R, D), F32)
    for start in range(0, K, 8):
        hidden = edge_forward(idx, table, part, slope, start, 8, hidden)
    h1, live = saved[0], live_in[...]
    new, inner, islope, n, scale = node_forward(h1, hidden, live, w, 1)
    du, da, back, dh1 = node_backward(cot[...], live, islope, n, scale, wt, 1)
    drecv = edge_terms(slope, back, terms)
    got = edge_scatter(idxt, terms, 0, 3)
    for xs, out in enumerate((pa0, pa1, pa2)):
        out[...] = got[xs * R : (xs + 1) * R]
    pb[...] = edge_scatter(idxt, terms, 6, 3).reshape(3, R, D)
    for i, value in enumerate((hidden, inner, du, da, drecv, dh1, new)):
        kept[i] = value


def middle_1_rest(
    flags, idxt, terms, kept, saved, w, wt, leave_rows, leave_counts,
    po, h_out, rows_keep, rows_send, g,
    h2, sem,
):
    hidden, inner, du, da, drecv, dh1, new = (kept[i] for i in range(7))
    h2[...] = new
    copy = pltpu.make_async_copy(h2, h_out, sem)
    copy.start()
    pack_leaving(flags, leave_rows, leave_counts, new, rows_keep, rows_send)
    po[...] = edge_scatter(idxt, terms, 3, 3).reshape(3, R, D)
    message = mm(hidden, w[1, EDGE])
    dmessage = mm(da, wt[1, NODE + 1])
    grads = weight_grads(saved[0], hidden, message, inner, du, da, dmessage, drecv)
    for i, value in enumerate(grads):
        g[i * D : (i + 1) * D] = value
    g[5 * D :] = dh1 + mm(drecv, wt[1, RECV])
    copy.wait()


def backward_0(
    idxt, ma, mo, mb, saved, slope_in, bins_in, g1, live, wt,
    pa, pb, po, sums, terms_out, bins,
    terms, slope, sems,
):
    copies = [
        pltpu.make_async_copy(src, dst, sems.at[i])
        for i, (src, dst) in enumerate(
            (
                (slope_in, slope),
                (bins_in, bins),
            )
        )
    ]
    for copy in copies:
        copy.start()
    dsend = ma[...] + mo[...] + mb[...]
    dh1 = g1[5 * D :] + mm(dsend, wt[1, SEND])
    du, da, back, dh0 = node_backward(dh1, live[...], saved[5], saved[6], saved[7][:, 0:1], wt, 0)
    copies[0].wait()
    drecv = edge_terms(slope, back, terms)
    got = edge_scatter(idxt, terms, 0, BLOCKS)
    for part, out in enumerate((pa, po, pb)):
        for xs in range(3):
            v = got[(part * 3 + xs) * R : (part * 3 + xs + 1) * R]
            sums[part * 3 + xs] = v
            out[xs] = mm(v, wt[0, SEND])
    po[1] += dh0 + mm(drecv, wt[0, RECV])
    terms_out[0] = du
    terms_out[1] = da
    terms_out[2] = drecv
    terms_out[3] = dsend
    for copy in copies[1:]:
        copy.wait()


def grads_0(flags, saved, bins, sums, parts, h, g1, wt, keep, *rest):
    *send, g = rest
    du, da, drecv, dsend = (parts[i] for i in range(4))
    dmessage = mm(da, wt[0, NODE + 1])
    total = mm_tn(bins[0], sums[0])
    for b in range(1, BLOCKS):
        total = total + mm_tn(bins[b], sums[b])
    g[0, 0:D] = total
    grads = weight_grads(h[...], saved[2], saved[3], saved[4], du, da, dmessage, drecv)
    for i, value in enumerate(grads):
        g[0, (i + 1) * D : (i + 2) * D] = value
    g[1, 0:D] = mm_tn(saved[0], dsend)
    g[1, D:] = g1[0 : 5 * D]
    mine = flags[2]
    keep[...] = g[mine]
    for out, first, last in zip(send, CUTS, CUTS[1:]):
        out[...] = g[1 - mine, first * PIECE : last * PIECE]


def pack_leaving(flags, rows, counts, h, keep, send):
    q = lax.broadcasted_iota(jnp.int32, (CAP, DEVICES), 0)
    rows = jnp.where(q < lax.broadcast_in_dim(counts[...], (CAP, DEVICES), (0, 1)), rows[...], -1)
    target = lax.broadcasted_iota(jnp.int32, (DEVICES, DEVICES), 0)
    at = lax.broadcasted_iota(jnp.int32, (DEVICES, DEVICES), 1)
    first = at < CHIPS
    wanted = jnp.where(first, 2 * at + flags[2], 2 * (at - CHIPS) + 1 - flags[2])
    order = jnp.where(target == wanted, 1.0, 0.0).astype(BF16)
    rows = jnp.dot(rows.astype(F32).astype(BF16), order, preferred_element_type=F32)
    rows = rows.astype(jnp.int32)
    paired = jnp.concatenate(halves(h), 1)
    slots = lax.broadcasted_iota(jnp.int32, (R, DEVICES), 0)
    for c in range(CAP):
        line = lax.broadcast_in_dim(rows[c : c + 1], (R, DEVICES), (0, 1))
        hot = jnp.where(slots == line, 1.0, 0.0).astype(BF16)
        got = fold(
            lax.dot_general(hot, paired, (((0,), (0,)), ((), ())), preferred_element_type=F32)
        )
        keep[c * CHIPS : (c + 1) * CHIPS] = got[:CHIPS]
        send[c * CHIPS : (c + 1) * CHIPS] = got[CHIPS:]


def tail_pack(flags, rows_keep, rows_got, g_keep, *rest):
    *g_got, out = rest
    even = flags[2] == 0
    for q in range(CAP):
        at = slice(q * CHIPS, (q + 1) * CHIPS)
        out[pl.ds(q, CHIPS, stride=EACH)] = jnp.where(even, rows_keep[at], rows_got[at])
        out[pl.ds(CAP + q, CHIPS, stride=EACH)] = jnp.where(even, rows_got[at], rows_keep[at])
    for got, first, last in zip(g_got, CUTS, CUTS[1:]):
        for i in range(first, last):
            near = got[(i - first) * PIECE : (i - first + 1) * PIECE]
            out[i * EACH + 2 * CAP : (i + 1) * EACH] = g_keep[i * PIECE : (i + 1) * PIECE] + near


def tail_sum(arrived, out):
    for q in range(PIECE):
        rows = arrived[pl.ds(2 * CAP + q, CHIPS, stride=EACH)]
        total = jnp.sum(rows, axis=0, keepdims=True)
        out[pl.ds(q, CHIPS, stride=PIECE)] = lax.broadcast_in_dim(total, (CHIPS, D), (0, 1))


def take_arrivals(arrived, out, rows, sem):
    for i in range(CHIPS):
        rows[i * 2 * CAP : (i + 1) * 2 * CAP] = arrived[i * EACH : i * EACH + 2 * CAP]
    copy = pltpu.make_async_copy(rows, out, sem)
    copy.start()
    copy.wait()


def tail_split(flags, own, other, o_send, o_recv, o_edge, o_node, o_update, sems):
    mine = flags[2]
    copies = []
    for out, at, size in (
        (o_send, 0, D),
        (o_recv, D, D),
        (o_edge, 2 * D, D),
        (o_node, 3 * D, 2 * D),
        (o_update, 5 * D, D),
    ):
        for rows, step in ((own, mine), (other, 1 - mine)):
            copies.append(
                pltpu.make_async_copy(rows.at[at : at + size], out.at[step], sems.at[len(copies)])
            )
            copies[-1].start()
    for copy in copies:
        copy.wait()


def vmem(*shape):
    return pltpu.VMEM(shape, F32)


def call(kernel, outs, scratch, args, microseconds=1.0):
    places = {"s": pltpu.SMEM, "v": pltpu.VMEM, "w": pltpu.VMEM, "h": pltpu.HBM, "a": pl.ANY}
    return pl.pallas_call(
        kernel,
        out_shape=[
            {"h": pltpu.HBM, "w": pltpu.VMEM, "v": jax.ShapeDtypeStruct}[p](shape, *(kind or (F32,)))
            for p, shape, *kind in outs
        ],
        in_specs=[pl.BlockSpec(memory_space=places[p]) for p, _ in args],
        out_specs=[pl.BlockSpec(memory_space=places[p]) for p, *_ in outs],
        scratch_shapes=scratch,
        compiler_params=pltpu.CompilerParams(vmem_limit_bytes=VMEM_BYTES),
        cost_estimate=pl.CostEstimate(
            flops=int(microseconds * 1e9), bytes_accessed=int(microseconds * 3e6), transcendentals=0
        ),
    )(
        *[
            pltpu.with_memory_space_constraint(a, places[p]) if p in "hw" else a
            for p, a in args
        ]
    )


def swap(a, axis, second):
    n = lax.axis_size(axis)
    if not second:
        return lax.ppermute(a, axis, [(i, i ^ 1) for i in range(n)])
    pairs = [(i, (i + 1) % n if i % 2 else (i - 1) % n) for i in range(n)]
    if axis == "gy":
        return lax.ppermute(a, axis, pairs)
    return lax.ppermute(
        a,
        AXES,
        [
            (x * GY + y, x * GY + (y ^ 1) if x in (0, n - 1) else to * GY + y)
            for x, to in pairs
            for y in range(GY)
        ],
    )


def neighbours_along_gx(own):
    return swap(own, "gx", False), swap(own, "gx", True)


def neighbours_along_gy(first, own, second):
    column = jnp.stack([first, own, second])
    return [swap(a, "gy", False) for a in (first, own, second)], column, swap(column, "gy", True)


def along_gy(pa, pb):
    return swap(pa, "gy", False), swap(pb, "gy", True)


def columns(ra, po, rb):
    return po[0] + ra[0] + rb[0], po[1] + ra[1] + rb[1], po[2] + ra[2] + rb[2]


def exchange(a):
    groups = [[2 * chip + core for chip in range(CHIPS)] for core in range(2)]
    moved = lax.all_to_all(
        a.reshape(CHIPS, 1, -1),
        AXES,
        split_axis=0,
        concat_axis=0,
        tiled=True,
        axis_index_groups=groups,
    )
    return moved.reshape(a.shape)


def body(
    initial_latents,
    final_cotangent,
    bin_counts,
    neighbours,
    leave_rows,
    leave_counts,
    w_send,
    w_receive,
    w_edge,
    w_node,
    w_update,
):
    gx, gy = lax.axis_index("gx"), lax.axis_index("gy")
    core = gy % 2
    flags = jnp.stack(
        [
            ((gx > 0) & (gx < GX - 1)).astype(jnp.int32),
            ((gy > 0) & (gy < GY - 1)).astype(jnp.int32),
            core,
            gx % 2,
        ]
    )
    raw = neighbours[0, 0].T
    row, table3, big, bins9 = (R, D), (3, R, D), (K, R, D), (BLOCKS, R, D)
    two, rows6, pairs = (2, R, D), (6 * D, D), (2, 7, 2 * D, 2 * D)
    terms = pltpu.VMEM((K * R, 2 * D), BF16)
    dma = pltpu.SemaphoreType.DMA
    masked, h0, live = call(
        mask_dead,
        [("v", row), ("w", row), ("w", row)],
        [pltpu.SMEM((1, 1), jnp.int32), dma((2,))],
        [("a", bin_counts), ("h", initial_latents[0, 0])],
    )
    first, second = neighbours_along_gx(masked)
    w, weights, idx, idxt, cot = call(
        prepare,
        [
            ("w", pairs, BF16), ("w", (2, 6 * D, D)), ("w", big, jnp.int32), ("w", (K, R), jnp.int32),
            ("w", row),
        ],
        [pltpu.VMEM((K, R), jnp.int32), dma((7,))],
        [
            ("s", flags), ("h", raw),
            ("h", w_send), ("h", w_receive), ("h", w_edge), ("h", w_node), ("h", w_update),
            ("h", final_cotangent[0, 0]),
        ],
    )
    first, second, w, idx = lax.optimization_barrier((first, second, w, idx))
    ta, to, tb = neighbours_along_gy(first, masked, second)
    half = pltpu.VMEM((3 * R, 2 * D), BF16)
    part, column_bins = call(
        column_0,
        [("w", big), ("w", table3)],
        [half],
        [("s", flags), ("v", to), ("w", idx), ("w", h0), ("w", w)],
    )
    part, partner_bins = call(
        partner_0,
        [("w", big), ("w", table3)],
        [half],
        [("s", flags), *(("v", a) for a in ta), ("w", idx), ("w", part), ("w", w)],
        1e-6,
    )
    send1, slope0, next_bins, kept = call(
        forward_0,
        [("v", row), ("w", big), ("w", table3), ("w", (6, R, D))],
        [half],
        [("s", flags), ("v", tb), ("w", idx), ("w", part), ("w", h0), ("w", live), ("w", w)],
    )
    slope0, bins0, saved = call(
        forward_0_rest,
        [("h", big), ("h", bins9), ("w", (8, R, D))],
        [dma((4,))],
        [("w", kept), ("w", slope0), ("w", partner_bins), ("w", column_bins), ("w", next_bins), ("w", w)],
    )
    first, second = neighbours_along_gx(send1)
    first, second, saved, weights = lax.optimization_barrier((first, second, saved, weights))
    ta, to, tb = neighbours_along_gy(first, send1, second)
    (wt,) = call(
        prepare_back, [("w", pairs, BF16)], [], [("w", weights), ("w", w)]
    )
    (part,) = call(
        column_1, [("w", big)], [half], [("s", flags), ("v", to), ("w", idx), ("w", saved)]
    )
    (part,) = call(
        partner_1, [("w", big)], [half], [("s", flags), *(("v", a) for a in ta), ("w", idx), ("w", part)], 1e-6
    )
    *pa, pb, terms1, kept = call(
        middle_1,
        [("v", row)] * 3 + [("v", table3), ("w", (K * R, 2 * D), BF16), ("w", (7, R, D))],
        [half, vmem(*big)],
        [
            ("s", flags), ("v", tb), ("w", idx), ("w", idxt), ("w", part), ("w", saved), ("w", cot),
            ("w", live), ("w", w), ("w", wt),
        ],
    )
    rb = swap(pb, "gy", True)
    ra = [swap(a, "gy", False) for a in pa]
    leave = (CHIPS * CAP, D)
    po, h2, rows_keep, rows_send, g1 = call(
        middle_1_rest,
        [("v", table3), ("h", row), ("w", leave), ("w", leave), ("w", rows6)],
        [vmem(*row), dma],
        [
            ("s", flags), ("w", idxt), ("w", terms1), ("w", kept), ("w", saved), ("w", w), ("w", wt),
            ("v", leave_rows[0, 0].T), ("v", leave_counts[0]),
        ],
    )
    rows_got = swap(rows_send, "gy", False)
    low, mo, high = columns(ra, po, rb)
    mb = swap(high, "gx", True)
    ma = swap(low, "gx", False)
    ma, mb, rows_got = lax.optimization_barrier((ma, mb, rows_got))
    pa, pb, po, sums0, parts0, bins0 = call(
        backward_0,
        [("w", table3), ("w", table3), ("w", table3), ("w", bins9), ("w", (4, R, D)), ("w", bins9)],
        [terms, vmem(*big), dma((2,))],
        [
            ("w", idxt), ("v", ma), ("v", mo), ("v", mb), ("w", saved), ("h", slope0),
            ("h", bins0), ("w", g1), ("w", live), ("w", wt),
        ],
    )
    g_keep, *g_send = call(
        grads_0,
        [("w", rows6)] + [("w", ((b - a) * PIECE, D)) for a, b in zip(CUTS, CUTS[1:])],
        [vmem(2, 6 * D, D)],
        [
            ("s", flags), ("w", saved), ("w", bins0), ("w", sums0), ("w", parts0), ("w", h0), ("w", g1), ("w", wt),
        ],
        5.0,
    )
    g_got = [swap(g, "gy", False) for g in g_send]
    ra, rb = along_gy(pa, pb)
    (outgoing,) = call(
        tail_pack,
        [("v", (CHIPS * EACH, D))],
        [],
        [("s", flags), ("v", rows_keep), ("v", rows_got), ("v", g_keep), *(("v", g) for g in g_got)],
        0.01,
    )
    outgoing, ra, rb = lax.optimization_barrier((outgoing, ra, rb))
    arrived = exchange(outgoing)
    (pieces,) = call(tail_sum, [("v", (CHIPS * PIECE, D))], [], [("v", arrived)])
    own = exchange(pieces)
    low, mid, high = columns(ra, po, rb)
    second = swap(high, "gx", True)
    first = swap(low, "gx", False)
    (arrivals,) = call(
        take_arrivals,
        [("h", (DEVICES * CAP, D))],
        [vmem(DEVICES * CAP, D), dma],
        [("v", arrived)],
    )
    own, first, second, arrivals = lax.optimization_barrier((own, first, second, arrivals))
    grad_initial = first + mid + second
    partner = swap(own, "gy", False)
    sums = call(
        tail_split,
        [("h", two), ("h", two), ("h", two), ("h", (2, 2 * D, D)), ("h", two)],
        [dma((10,))],
        [("s", flags), ("v", own), ("v", partner)],
    )
    return (
        h2.reshape(1, 1, R, D),
        arrivals.reshape(1, 1, DEVICES, CAP, D),
        grad_initial.reshape(1, 1, R, D),
        *sums,
    )


def solution(mesh):
    in_specs = (
        P("gx", "gy", None, None),
        P("gx", "gy", None, None),
        P("gx", "gy"),
        P("gx", "gy", None, None),
        P("gx", "gy", None, None),
        P("gx", "gy", None),
        P(),
        P(),
        P(),
        P(),
        P(),
    )
    out_specs = (
        P("gx", "gy", None, None),
        P("gx", "gy", None, None, None),
        P("gx", "gy", None, None),
        P(),
        P(),
        P(),
        P(),
        P(),
    )
    return jax.shard_map(body, mesh=mesh, in_specs=in_specs, out_specs=out_specs, check_vma=False)
```
